128 devices in a mesh: dp: 16 (over x, z_lo, core), expert: 8 (over y, z_hi).
Axes of the slice: x: 4, y: 4, z: 4 (z_hi: 2, z_lo: 2; z = z_hi * 2 + z_lo), core: 2. Of those that a mesh axis runs over, the one named last changes fastest.
Arguments:
- tokens: bfloat16 [1024, 7168], P(('dp', 'expert')), may hold values from -6 to 6
- assign: int32 [1024, 1], P(('dp', 'expert')), may hold values from 0 to 7; in each aligned block of 8 rows (0 to 7, 8 to 15, ...) at most 2 rows name the same one
- copy_share: int32 [128, 8], P(('dp', 'expert')), may hold values from 0 to 2
- copy_plan: int32 [8], replicated, may hold values from 0 to 7, as said below
- grad_out: bfloat16 [1024, 7168], P(('dp', 'expert')), may hold values from -6 to 6
- w_gate: bfloat16 [8, 7168, 2048], P('expert', None, 'dp'), may hold values from -0.0625 to 0.0625
- w_up: bfloat16 [8, 7168, 2048], P('expert', None, 'dp'), may hold values from -0.0625 to 0.0625
- w_down: bfloat16 [8, 2048, 7168], P('expert', 'dp'), may hold values from -0.125 to 0.125
Outputs:
- mixed: bfloat16 [1024, 7168], P(('dp', 'expert'))
- grad_in: bfloat16 [1024, 7168], P(('dp', 'expert'))
- grad_gate_w: bfloat16 [8, 7168, 2048], P('expert', None, 'dp')
- grad_up_w: bfloat16 [8, 7168, 2048], P('expert', None, 'dp')
- grad_down_w: bfloat16 [8, 2048, 7168], P('expert', 'dp')
- copy_grad_gate: bfloat16 [8, 7168, 2048], P('expert', None, 'dp')
- copy_grad_up: bfloat16 [8, 7168, 2048], P('expert', None, 'dp')
- copy_grad_down: bfloat16 [8, 2048, 7168], P('expert', 'dp')
The draws below stay inside these ranges and needn't reach their ends.
Inputs may be any that keep to these rules, and one draw needn't show every extreme that they name: `assign`: among the rows of one device no expert is named more than 2 times. `copy_plan`: each expert number appears exactly once.
All inputs are finite; a program needn't handle non-finite values.
Results may differ from the reference program's by a relative error of at most 0.0051.
Values may be sent and summed in bfloat16 or wider, within the bound.
A program may use at most 192 MiB of HBM per device.

```python
import math
import jax
import jax.numpy as jnp
import numpy as np
from jax import lax

D = 7168
FF = 2048
TOK_DEV = 8
EXPERTS = 8
CAP = 2
ROUTERS = 128
TOKENS = 1024


def draw_copy_share(key, part):
    key = jax.random.fold_in(key, 11)
    key_values, key_marked = jax.random.split(key)
    values = jax.random.randint(key_values, (ROUTERS, EXPERTS), 0, CAP + 1, dtype=jnp.int32)
    marked = jax.random.randint(key_marked, (), 0, ROUTERS * EXPERTS, dtype=jnp.int32)
    places = jnp.arange(ROUTERS * EXPERTS, dtype=jnp.int32).reshape(ROUTERS, EXPERTS)
    return jnp.where(places == marked, CAP, values).astype(jnp.int32)


def draw_copy_plan(key, part):
    key = jax.random.fold_in(key, 23)
    return jax.random.permutation(key, EXPERTS).astype(jnp.int32)


def block_scale(stream_key, dims, shards, low, high):
    loudness = 1.0
    for position, parts in shards:
        draws = jax.random.uniform(jax.random.fold_in(jax.random.fold_in(stream_key, 6), position), (parts,), jnp.float32, low / len(shards), high / len(shards))
        loudness = loudness * jnp.repeat(jnp.exp(draws), dims[position] // parts).reshape((-1,) + (1,) * (len(dims) - 1 - position))
    return loudness


def assign_block(own_key, own, number, rows, number_of, top, most, lean):
    order = jax.random.permutation(own_key, number_of)
    crowded, usual = shares(number_of, rows * top, most, lean, True), shares(number_of, rows * top, most, lean, False)
    places = jnp.arange(number_of)

    def named(sizes, rotation):
        used = int((sizes > 0).sum())
        fixed = max(1, used // 4)
        shifted = fixed + (places - fixed + rotation * (used - fixed)) % max(1, number_of - fixed)
        return jnp.zeros((number_of,), jnp.int32).at[order[jnp.where(places < fixed, places, shifted)]].set(jnp.asarray(sizes, jnp.int32))

    sizes = jnp.where(number % 4 == 0, named(crowded, number // 4), named(usual, number - number // 4 - 1))
    mixed = jax.random.permutation(jax.random.fold_in(own, 3), number_of)
    donor, taker = mixed[0:number_of // 2 * 2:2], mixed[1:number_of // 2 * 2:2]
    room = jnp.minimum(sizes[donor] - 1, most - sizes[taker]) // 2
    room = jnp.where((donor == order[0]) | (taker == order[0]) | (sizes[taker] == 0), 0, jnp.maximum(room, 0))
    shifted = jax.random.randint(jax.random.fold_in(own, 4), (number_of // 2,), 0, 1 << 20) % (room + 1)
    sizes = sizes.at[donor].add(-shifted).at[taker].add(shifted)
    items = jnp.searchsorted(jnp.cumsum(sizes), jnp.arange(rows * top), side="right").astype(jnp.int32)
    table = items.reshape(top, rows).T
    table = table[jax.random.permutation(jax.random.fold_in(own, 1), rows)]
    rotation = jax.random.randint(jax.random.fold_in(own, 2), (rows, 1), 0, top)
    return jnp.take_along_axis(table, (jnp.arange(top)[None, :] + rotation) % top, axis=1)


def shares(number_of, total, limit, lean, full):
    loads = [(1 << 20) // math.isqrt(rank ** lean) + 1 for rank in range(1, number_of + 1)]
    largest = limit if full else min(limit, max(-(-total // number_of), total * loads[0] // sum(loads)))
    least = 1 if total - largest >= number_of - 1 else 0
    counts, surplus = [largest] + [least] * (number_of - 1), total - largest - least * (number_of - 1)
    while surplus > 0:
        movable = [i for i in range(1, number_of) if counts[i] < largest] or [i for i in range(1, number_of) if counts[i] < limit]
        whole, left = sum([loads[i] for i in movable]), surplus
        for i in movable:
            addition = min(limit - counts[i], max(1, left * loads[i] // whole), surplus)
            counts[i] = counts[i] + addition
            surplus = surplus - addition
    return np.array(counts)


def scatter_about(key, extent, deviation, bound, cuts=(), kind=jnp.bfloat16):
    array = jax.random.normal(key, extent, jnp.float32) * deviation
    if len(cuts) > 0:
        array = block_scale(key, extent, cuts, -0.22, 0.18) * array
    return jnp.clip(array, min=-bound, max=bound).astype(kind)


def setup_inputs(seed: int = 0) -> dict:
    arg_keys = jax.random.split(jax.random.key(seed), 9)
    tokens = scatter_about(arg_keys[0], (TOKENS, D), 1.0, 6.0, ((0, 128),))
    assign_keys = jax.random.split(jax.random.fold_in(arg_keys[1], 1), TOKENS // TOK_DEV)
    assign_turns = jax.random.permutation(jax.random.fold_in(arg_keys[1], 3), TOKENS // TOK_DEV)
    assign = jax.vmap(lambda own, number: assign_block(jax.random.fold_in(arg_keys[1], 2), own, number, TOK_DEV, EXPERTS, 1, CAP, 2))(assign_keys, assign_turns).reshape((TOKENS, 1))
    copy_share = draw_copy_share(jax.random.fold_in(arg_keys[8], 71), 0)
    copy_plan = draw_copy_plan(jax.random.fold_in(arg_keys[8], 71), 0)
    grad_out = scatter_about(arg_keys[4], (TOKENS, D), 1.0, 6.0, ((0, 128),))
    w_gate = scatter_about(arg_keys[5], (EXPERTS, D, FF), D ** -0.5, 0.0625, ((0, 8), (2, 16)))
    w_up = scatter_about(arg_keys[6], (EXPERTS, D, FF), D ** -0.5, 0.0625, ((0, 8), (2, 16)))
    w_down = scatter_about(arg_keys[7], (EXPERTS, FF, D), FF ** -0.5, 0.125, ((0, 8), (1, 16)))
    return {"tokens": tokens, "assign": assign, "copy_share": copy_share, "copy_plan": copy_plan, "grad_out": grad_out, "w_gate": w_gate, "w_up": w_up, "w_down": w_down}


def expert_pass(number, expert_of, to_copy, tokens, grad_out, w_gate, w_up, w_down):
    most_rows = min(TOKENS, ROUTERS * CAP)
    picked = jnp.argsort((expert_of != number).astype(jnp.int32), stable=True)[:most_rows].astype(jnp.int32)
    valid = expert_of[picked] == number
    copied = jnp.logical_and(valid, to_copy[picked])[:, None]
    kept = jnp.logical_and(valid, jnp.logical_not(to_copy[picked]))[:, None]
    zero = jnp.zeros((), jnp.bfloat16)
    rows = jnp.where(valid[:, None], tokens[picked], zero).astype(jnp.bfloat16)
    backs = jnp.where(valid[:, None], grad_out[picked], zero).astype(jnp.bfloat16)
    weight_gate = w_gate[number]
    weight_up = w_up[number]
    weight_down = w_down[number]
    gate = jnp.dot(rows, weight_gate, preferred_element_type=jnp.float32)
    up = jnp.dot(rows, weight_up, preferred_element_type=jnp.float32)
    squash = jax.nn.sigmoid(gate)
    hidden = (gate * squash * up).astype(jnp.bfloat16)
    mixed = jnp.dot(hidden, weight_down, preferred_element_type=jnp.float32).astype(jnp.bfloat16)
    grad_hidden = jnp.dot(backs, weight_down.T, preferred_element_type=jnp.float32)
    grad_gate = (grad_hidden * up * squash * (1.0 + gate * (1.0 - squash))).astype(jnp.bfloat16)
    grad_upv = (grad_hidden * gate * squash).astype(jnp.bfloat16)
    rows_kept = jnp.where(kept, rows, zero).astype(jnp.bfloat16)
    rows_copied = jnp.where(copied, rows, zero).astype(jnp.bfloat16)
    backs_kept = jnp.where(kept, backs, zero).astype(jnp.bfloat16)
    backs_copied = jnp.where(copied, backs, zero).astype(jnp.bfloat16)
    down_kept = jnp.dot(hidden.T, backs_kept, preferred_element_type=jnp.float32).astype(jnp.bfloat16)
    down_copied = jnp.dot(hidden.T, backs_copied, preferred_element_type=jnp.float32).astype(jnp.bfloat16)
    gate_kept = jnp.dot(rows_kept.T, grad_gate, preferred_element_type=jnp.float32).astype(jnp.bfloat16)
    gate_copied = jnp.dot(rows_copied.T, grad_gate, preferred_element_type=jnp.float32).astype(jnp.bfloat16)
    up_kept = jnp.dot(rows_kept.T, grad_upv, preferred_element_type=jnp.float32).astype(jnp.bfloat16)
    up_copied = jnp.dot(rows_copied.T, grad_upv, preferred_element_type=jnp.float32).astype(jnp.bfloat16)
    grad_rows = (jnp.dot(grad_gate, weight_gate.T, preferred_element_type=jnp.float32) + jnp.dot(grad_upv, weight_up.T, preferred_element_type=jnp.float32)).astype(jnp.bfloat16)
    return (picked, mixed, grad_rows, gate_kept, up_kept, down_kept, gate_copied, up_copied, down_copied)


def reference(tokens, assign, copy_share, copy_plan, grad_out, w_gate, w_up, w_down):
    expert_of = assign[:, 0]
    grouped = expert_of.reshape(ROUTERS, TOK_DEV)
    numbers = jnp.arange(EXPERTS, dtype=jnp.int32)
    onehot = (grouped[:, :, None] == numbers[None, None, :]).astype(jnp.int32)
    rank_in = jnp.sum((jnp.cumsum(onehot, axis=1) - onehot) * onehot, axis=2)
    limit_rows = jnp.sum(copy_share[:, None, :] * onehot, axis=2)
    to_copy = (rank_in < limit_rows).reshape(-1)

    def one(number):
        return expert_pass(number, expert_of, to_copy, tokens, grad_out, w_gate, w_up, w_down)

    results = lax.map(one, jnp.arange(EXPERTS, dtype=jnp.int32))
    picked, mixed, grad_rows, gate_kept, up_kept, down_kept, gate_copied, up_copied, down_copied = results
    index = picked.reshape(-1)
    out_rows = jnp.zeros((TOKENS, D), jnp.float32).at[index].add(mixed.reshape(-1, D).astype(jnp.float32))
    in_rows = jnp.zeros((TOKENS, D), jnp.float32).at[index].add(grad_rows.reshape(-1, D).astype(jnp.float32))
    copy_gate = jnp.take(gate_copied, copy_plan, axis=0)
    copy_up = jnp.take(up_copied, copy_plan, axis=0)
    copy_down = jnp.take(down_copied, copy_plan, axis=0)
    return (out_rows.astype(jnp.bfloat16), in_rows.astype(jnp.bfloat16), gate_kept, up_kept, down_kept, copy_gate, copy_up, copy_down)
```

```python
import functools

import jax
import jax.numpy as jnp
from jax import lax
from jax.experimental import pallas as pl
from jax.experimental.pallas import tpu as pltpu
from jax.sharding import PartitionSpec as P

MESH = pl.DeviceIdType.MESH
BF16 = jnp.bfloat16
F32 = jnp.float32
LANES = 128


def dot(a, b):
    return jnp.dot(a, b, preferred_element_type=F32)


def dot_nt(a, b):
    return lax.dot_general(a, b, (((1,), (1,)), ((), ())), preferred_element_type=F32)


def dot_tn(a, b):
    return lax.dot_general(a, b, (((0,), (0,)), ((), ())), preferred_element_type=F32)


def kernel(
    experts,
    half,
    part_p,
    chunk,
    plan_ref,
    ext_ref,
    w_gate,
    w_up,
    w_down,
    o_out,
    gate_out,
    up_out,
    down_out,
    copy_gate_out,
    copy_up_out,
    copy_down_out,
    raw,
    a2a_send,
    a2a_recv,
    own,
    cpy,
    w1,
    wd,
    pre,
    pre_recv,
    acts,
    gx1,
    gx2s,
    gx2,
    gcat,
    hcat,
    part,
    rz,
    rxo,
    rxf,
    ro_q,
    rf_q,
    rzq,
    fin,
    back_send,
    back_recv,
    outs,
    st1,
    st2,
    ct1,
    ct2,
    ssem,
    rsem,
    lsem,
):
    units = w1.shape[2] // 2
    full = half + LANES
    per_chip = 4 * experts
    slots = 8 * per_chip
    block = 2 * per_chip
    mid = block // 2
    steps = half // chunk
    part_q = half - part_p

    dp = lax.axis_index("dp")
    ex = lax.axis_index("expert")
    x = dp // 4
    z = (dp // 2) % 2
    c = dp % 2
    o = 1 - c

    def chip(dx, zz):
        return lax.rem(x + dx, 4) * 2 + zz

    me = chip(0, z)
    xp = (lax.rem(dp + 4, 16), ex)
    xm = (lax.rem(dp + 12, 16), ex)
    zp = (dp + 2 - 4 * z, ex)
    sib = (dp + 1 - 2 * c, ex)

    def peer(i):
        return (dp, lax.rem(ex + i, experts))

    used = [0]
    sends = []

    def fresh():
        used[0] += 1
        return used[0] - 1

    def msg(k, src, dst, dev):
        copy = pltpu.make_async_remote_copy(
            src_ref=src,
            dst_ref=dst,
            send_sem=ssem.at[k],
            recv_sem=rsem.at[k],
            device_id=dev,
            device_id_type=MESH,
        )
        copy.start()
        sends.append(copy)

    def got(k, ref, dev):
        pltpu.make_async_remote_copy(
            src_ref=ref,
            dst_ref=ref,
            send_sem=ssem.at[k],
            recv_sem=rsem.at[k],
            device_id=dev,
            device_id_type=MESH,
        ).wait_recv()

    used_local = [0]

    def local(src, dst):
        copy = pltpu.make_async_copy(src, dst, lsem.at[used_local[0]])
        used_local[0] += 1
        copy.start()
        return copy

    my_rows = pl.ds(pl.multiple_of(c * half, half), half)
    other_rows = pl.ds(pl.multiple_of(o * half, half), half)

    weight_loads = [
        local(w_gate.at[0, my_rows, :], w1.at[0, :, pl.ds(0, units)]),
        local(w_up.at[0, my_rows, :], w1.at[0, :, pl.ds(units, units)]),
        local(w_down.at[0, :, my_rows], wd.at[pl.ds(0, units), :]),
    ]

    barrier = pltpu.get_barrier_semaphore()
    greeted = [xp, xm, zp, sib] + [peer(i) for i in range(1, experts)]
    for dev in greeted:
        pl.semaphore_signal(barrier, inc=1, device_id=dev, device_id_type=MESH)
    pl.semaphore_wait(barrier, len(greeted))

    k_raw = fresh()
    msg(k_raw, ext_ref.at[o], raw.at[c], sib)
    k_w = [fresh() for _ in range(3)]
    msg(k_w[0], w_gate.at[0, other_rows, :], w1.at[1, :, pl.ds(0, units)], sib)
    msg(k_w[1], w_up.at[0, other_rows, :], w1.at[1, :, pl.ds(units, units)], sib)
    msg(k_w[2], w_down.at[0, :, other_rows], wd.at[pl.ds(units, units), :], sib)
    raw[c] = ext_ref[c]
    got(k_raw, raw.at[o], sib)

    placed = raw[:, :, half:full].reshape(32, LANES)[:, : 16 * experts]
    rows = raw[...].reshape(32, full)
    a2a_send[...] = dot_tn(placed, rows).astype(BF16).reshape(experts, 16, full)
    k_a2a = [fresh() for _ in range(experts - 1)]
    for i in range(1, experts):
        dev = peer(i)
        msg(k_a2a[i - 1], a2a_send.at[dev[1]], a2a_recv.at[ex], dev)
    a2a_recv[ex] = a2a_send[ex]
    for i in range(1, experts):
        got(k_a2a[i - 1], a2a_recv.at[lax.rem(ex + experts - i, experts)], peer(i))

    size = 16 * experts
    to = lax.broadcasted_iota(jnp.int32, (size, size), 0)
    fr = lax.broadcasted_iota(jnp.int32, (size, size), 1)
    want = (
        ((fr // 8) % 2) * block + ((fr // 4) % 2) * per_chip + (fr // 16) * 4 + fr % 4
    )
    moved = dot((to == want).astype(BF16), a2a_recv[...].reshape(size, full)).astype(BF16)
    own[me] = moved[:block]
    cpy[me] = moved[block:, :half]

    def gather(buf, width):
        keys = [fresh() for _ in range(18)]

        def cut(q, lane, row=None):
            start, count = (0, block) if row is None else (row * mid, mid)
            if lane == 0:
                return buf.at[q, pl.ds(start, count), pl.ds(0, part_p)]
            return buf.at[q, pl.ds(start, count), pl.ds(part_p, width - part_p)]

        y = 1 - z

        def first():
            msg(keys[9], cut(me, 1), cut(me, 1), zp)
            msg(keys[0], cut(me, 0), cut(me, 0), xp)
            msg(keys[1], cut(me, 0), cut(me, 0), xm)
            msg(keys[2], cut(me, 0), cut(me, 0), zp)
            msg(keys[10], cut(me, 1), cut(me, 1), xp)
            msg(keys[11], cut(me, 1), cut(me, 1), xm)

        def second():
            got(keys[9], cut(chip(0, y), 1), zp)
            msg(keys[12], cut(chip(0, y), 1), cut(chip(0, y), 1), xp)
            msg(keys[13], cut(chip(0, y), 1), cut(chip(0, y), 1), xm)
            got(keys[0], cut(chip(3, z), 0), xm)
            msg(keys[3], cut(chip(3, z), 0, 0), cut(chip(3, z), 0, 0), xp)
            msg(keys[5], cut(chip(3, z), 0), cut(chip(3, z), 0), zp)
            got(keys[1], cut(chip(1, z), 0), xp)
            msg(keys[4], cut(chip(1, z), 0, 1), cut(chip(1, z), 0, 1), xm)
            msg(keys[6], cut(chip(1, z), 0), cut(chip(1, z), 0), zp)

        def third():
            got(keys[10], cut(chip(3, z), 1), xm)
            msg(keys[14], cut(chip(3, z), 1, 0), cut(chip(3, z), 1, 0), xp)
            got(keys[11], cut(chip(1, z), 1), xp)
            msg(keys[15], cut(chip(1, z), 1, 1), cut(chip(1, z), 1, 1), xm)
            got(keys[3], cut(chip(2, z), 0, 0), xm)
            msg(keys[7], cut(chip(2, z), 0, 0), cut(chip(2, z), 0, 0), zp)
            got(keys[4], cut(chip(2, z), 0, 1), xp)
            msg(keys[8], cut(chip(2, z), 0, 1), cut(chip(2, z), 0, 1), zp)
            got(keys[12], cut(chip(3, y), 1), xm)
            msg(keys[16], cut(chip(3, y), 1, 0), cut(chip(3, y), 1, 0), xp)
            got(keys[13], cut(chip(1, y), 1), xp)
            msg(keys[17], cut(chip(1, y), 1, 1), cut(chip(1, y), 1, 1), xm)

        def last():
            got(keys[2], cut(chip(0, y), 0), zp)
            got(keys[5], cut(chip(3, y), 0), zp)
            got(keys[6], cut(chip(1, y), 0), zp)
            got(keys[14], cut(chip(2, z), 1, 0), xm)
            got(keys[15], cut(chip(2, z), 1, 1), xp)
            got(keys[7], cut(chip(2, y), 0, 0), zp)
            got(keys[8], cut(chip(2, y), 0, 1), zp)
            got(keys[16], cut(chip(2, y), 1, 0), xm)
            got(keys[17], cut(chip(2, y), 1, 1), xp)

        return first, second, third, last

    own_first, own_second, own_third, own_last = gather(own, full)
    cpy_first, cpy_second, cpy_third, cpy_last = gather(cpy, half)
    own_first()
    own_second()
    own_third()
    cpy_first()

    for load in weight_loads:
        load.wait()
    got(k_w[0], w1.at[1, :, pl.ds(0, units)], sib)
    got(k_w[1], w1.at[1, :, pl.ds(units, units)], sib)
    got(k_w[2], wd.at[pl.ds(units, units), :], sib)
    own_last()

    pre[...] = jnp.zeros_like(pre)

    def tokens_of(buf, cols):
        return buf[:, :per_chip, cols].reshape(slots, chunk)

    def backs_of(buf, cols):
        return buf[:, per_chip:, cols].reshape(slots, chunk)

    @pl.loop(0, steps)
    def _(step):
        cols = pl.ds(pl.multiple_of(step * chunk, chunk), chunk)
        t = tokens_of(own, cols)
        g = backs_of(own, cols)
        pre[0, :, : 2 * units] += dot(t, w1[0, cols, :])
        pre[1, :, : 2 * units] += dot(t, w1[1, cols, :])
        gh = dot_nt(g, wd[:, cols])
        pre[0, :, 2 * units :] += gh[:, :units]
        pre[1, :, 2 * units :] += gh[:, units:]

    k_pre = fresh()
    msg(k_pre, pre.at[1], pre_recv, sib)
    cpy_second()
    got(k_pre, pre_recv, sib)
    total = pre[0] + pre_recv[...]
    gate = total[:, :units]
    up = total[:, units : 2 * units]
    grad_hidden = total[:, 2 * units :]
    squash = jax.nn.sigmoid(gate)
    acts[0, :, :units] = (gate * squash * up).astype(BF16)
    acts[0, :, units : 2 * units] = (
        grad_hidden * up * squash * (1.0 + gate * (1.0 - squash))
    ).astype(BF16)
    acts[0, :, 2 * units :] = (grad_hidden * gate * squash).astype(BF16)
    k_acts = fresh()
    msg(k_acts, acts.at[0], acts.at[1], sib)

    k_gx1 = [fresh() for _ in range(experts - 1)]
    for i in range(1, experts):
        dev = peer(i)
        piece = pl.ds(pl.multiple_of(dev[1] * (slots // experts), slots // experts), slots // experts)
        msg(k_gx1[i - 1], acts.at[0, piece, :], gx1.at[ex], dev)
    piece = pl.ds(pl.multiple_of(ex * (slots // experts), slots // experts), slots // experts)
    gx1[ex] = acts[0, piece, :]

    got(k_acts, acts.at[1], sib)
    hcat[:, :units] = acts[0, :, :units]
    hcat[:, units:] = acts[1, :, :units]

    @pl.loop(0, steps)
    def _(step):
        cols = pl.ds(pl.multiple_of(step * chunk, chunk), chunk)
        m = dot(hcat[...], wd[:, cols])
        part[:, :per_chip, cols] = m.astype(BF16).reshape(8, per_chip, chunk)
        r = dot_nt(acts[0, :, units:], w1[0, cols, :]) + dot_nt(acts[1, :, units:], w1[1, cols, :])
        part[:, per_chip:, cols] = r.astype(BF16).reshape(8, per_chip, chunk)

    cols_p = pl.ds(0, part_p)
    cols_q = pl.ds(part_p, part_q)
    first_rows = pl.ds(0, mid)
    last_rows = pl.ds(mid, mid)
    every = pl.ds(0, block)
    y = 1 - z

    k_z = [fresh() for _ in range(4)]
    k_xo = [fresh() for _ in range(2)]
    k_xf = [fresh() for _ in range(2)]
    k_yo = [[fresh() for _ in range(2)] for _ in range(2)]
    k_yf = [[fresh() for _ in range(2)] for _ in range(2)]
    k_w0 = fresh()

    def add(ref, extra):
        ref[...] = (ref[...].astype(F32) + extra[...].astype(F32)).astype(BF16)

    for j in (2, 1, 3, 0):
        msg(k_z[j], part.at[chip(j, y), every, cols_p], rz.at[j], zp)
    for i, zz in enumerate((y, z)):
        msg(k_yo[i][0], part.at[chip(2, zz), first_rows, cols_q], ro_q.at[i, 0], xp)
        msg(k_yo[i][1], part.at[chip(2, zz), last_rows, cols_q], ro_q.at[i, 1], xm)
    cpy_third()

    for i in range(1, experts):
        got(k_gx1[i - 1], gx1.at[lax.rem(ex + experts - i, experts)], peer(i))
    for i in range(experts):
        gx2s[i] = gx1[plan_ref[i]]
    k_gx2 = [fresh() for _ in range(experts - 1)]
    for i in range(1, experts):
        dev = peer(i)
        msg(k_gx2[i - 1], gx2s.at[dev[1]], gx2.at[0, ex], dev)
    gx2[0, ex] = gx2s[ex]

    marks = own[:, :per_chip, half:full].reshape(slots, LANES).astype(F32)
    lane = lax.broadcasted_iota(jnp.int32, (slots, LANES), 1)
    copied = jnp.sum(jnp.where((lane // 8) % 2 == 1, marks, 0.0), axis=1, keepdims=True)
    kept = 1.0 - copied
    gcat[:, : 2 * units] = (acts[0, :, units:].astype(F32) * kept).astype(BF16)
    gcat[:, 2 * units :] = (acts[1, :, units:].astype(F32) * kept).astype(BF16)
    hcat[...] = (hcat[...].astype(F32) * kept).astype(BF16)

    def weight_grads(buf, one, two):
        @pl.loop(0, steps)
        def _(step):
            cols = pl.ds(pl.multiple_of(step * chunk, chunk), chunk)
            d = dot_tn(tokens_of(buf, cols), gcat[...]).astype(BF16)
            one[0, cols, :] = d[:, : 2 * units]
            one[1, cols, :] = d[:, 2 * units :]
            two[:, cols] = dot_tn(hcat[...], backs_of(buf, cols)).astype(BF16)

    def write_grads(one, two, g_out, u_out, d_out):
        keys = [fresh() for _ in range(3)]
        lanes_g, lanes_u = pl.ds(0, units), pl.ds(units, units)
        msg(keys[0], one.at[1, :, lanes_g], g_out.at[0, my_rows, :], sib)
        msg(keys[1], one.at[1, :, lanes_u], u_out.at[0, my_rows, :], sib)
        msg(keys[2], two.at[lanes_u, :], d_out.at[0, :, my_rows], sib)
        mine = [
            local(one.at[0, :, lanes_g], g_out.at[0, my_rows, :]),
            local(one.at[0, :, lanes_u], u_out.at[0, my_rows, :]),
            local(two.at[lanes_g, :], d_out.at[0, :, my_rows]),
        ]

        def finish():
            for copy in mine:
                copy.wait()
            got(keys[0], g_out.at[0, other_rows, :], sib)
            got(keys[1], u_out.at[0, other_rows, :], sib)
            got(keys[2], d_out.at[0, :, other_rows], sib)

        return finish

    weight_grads(own, st1, st2)
    finish_own = write_grads(st1, st2, gate_out, up_out, down_out)

    for i, zz in enumerate((y, z)):
        got(k_yo[i][0], ro_q.at[i, 0], xm)
        add(part.at[chip(1, zz), first_rows, cols_q], ro_q.at[i, 0])
        msg(k_yf[i][0], part.at[chip(1, zz), every, cols_q], rf_q.at[i, 0], xp)
        got(k_yo[i][1], ro_q.at[i, 1], xp)
        add(part.at[chip(3, zz), last_rows, cols_q], ro_q.at[i, 1])
        msg(k_yf[i][1], part.at[chip(3, zz), every, cols_q], rf_q.at[i, 1], xm)
    got(k_z[2], rz.at[2], zp)
    add(part.at[chip(2, z), every, cols_p], rz.at[2])
    msg(k_xo[0], part.at[chip(2, z), first_rows, cols_p], rxo.at[0], xp)
    msg(k_xo[1], part.at[chip(2, z), last_rows, cols_p], rxo.at[1], xm)
    got(k_z[1], rz.at[1], zp)
    add(part.at[chip(1, z), every, cols_p], rz.at[1])
    got(k_z[3], rz.at[3], zp)
    add(part.at[chip(3, z), every, cols_p], rz.at[3])
    got(k_xo[0], rxo.at[0], xm)
    add(part.at[chip(1, z), first_rows, cols_p], rxo.at[0])
    msg(k_xf[0], part.at[chip(1, z), every, cols_p], rxf.at[0], xp)
    got(k_xo[1], rxo.at[1], xp)
    add(part.at[chip(3, z), last_rows, cols_p], rxo.at[1])
    msg(k_xf[1], part.at[chip(3, z), every, cols_p], rxf.at[1], xm)

    got(k_yf[0][0], rf_q.at[0, 0], xm)
    got(k_yf[0][1], rf_q.at[0, 1], xp)
    mine_y = part.at[chip(0, y), every, cols_q]
    mine_y[...] = (
        mine_y[...].astype(F32) + rf_q[0, 0].astype(F32) + rf_q[0, 1].astype(F32)
    ).astype(BF16)
    msg(k_w0, mine_y, rzq, zp)

    cpy_last()
    for i in range(1, experts):
        got(k_gx2[i - 1], gx2.at[0, lax.rem(ex + experts - i, experts)], peer(i))
    k_gsib = fresh()
    msg(k_gsib, gx2.at[0], gx2.at[1], sib)

    got(k_z[0], rz.at[0], zp)
    got(k_xf[0], rxf.at[0], xm)
    got(k_xf[1], rxf.at[1], xp)
    fin[:, cols_p] = (
        part[me, :, cols_p].astype(F32)
        + rz[0].astype(F32)
        + rxf[0].astype(F32)
        + rxf[1].astype(F32)
    ).astype(BF16)
    got(k_yf[1][0], rf_q.at[1, 0], xm)
    got(k_yf[1][1], rf_q.at[1, 1], xp)
    got(k_w0, rzq, zp)
    fin[:, cols_q] = (
        part[me, :, cols_q].astype(F32)
        + rf_q[1, 0].astype(F32)
        + rf_q[1, 1].astype(F32)
        + rzq[...].astype(F32)
    ).astype(BF16)

    to = lax.broadcasted_iota(jnp.int32, (size, block), 0)
    fr = lax.broadcasted_iota(jnp.int32, (size, block), 1)
    want = (to // 16) * 4 + ((to // 4) % 2) * per_chip + to % 4
    side = (to // 8) % 2
    quarter = half // 2
    back_send[...] = (
        dot(jnp.logical_and(fr == want, side == 0).astype(BF16), fin[:, :quarter])
        + dot(jnp.logical_and(fr == want, side == 1).astype(BF16), fin[:, quarter:])
    ).astype(BF16).reshape(experts, 16, quarter)
    k_back = [fresh() for _ in range(experts - 1)]
    for i in range(1, experts):
        dev = peer(i)
        msg(k_back[i - 1], back_send.at[dev[1]], back_recv.at[ex], dev)
    back_recv[ex] = back_send[ex]

    got(k_gsib, gx2.at[1], sib)
    for i in range(2):
        gcat[:, 2 * units * i : 2 * units * (i + 1)] = gx2[i, :, :, units:].reshape(
            slots, 2 * units
        )
        hcat[:, units * i : units * (i + 1)] = gx2[i, :, :, :units].reshape(slots, units)
    weight_grads(cpy, ct1, ct2)
    finish_cpy = write_grads(ct1, ct2, copy_gate_out, copy_up_out, copy_down_out)

    for i in range(1, experts):
        got(k_back[i - 1], back_recv.at[lax.rem(ex + experts - i, experts)], peer(i))
    spots = raw[:, :, half:full].reshape(32, LANES).astype(F32)
    lane = lax.broadcasted_iota(jnp.int32, (32, LANES), 1)
    spots = jnp.where((lane // 8) % 2 == 0, spots, 0.0)
    later = pltpu.roll(spots, 8, 1)
    got_back = back_recv[...].reshape(size, quarter)
    outs[:, :, :quarter] = (
        dot(spots[:, :size].astype(BF16), got_back).astype(BF16).reshape(2, 16, quarter)
    )
    outs[:, :, quarter:] = (
        dot(later[:, :size].astype(BF16), got_back).astype(BF16).reshape(2, 16, quarter)
    )
    k_out = fresh()
    msg(k_out, outs.at[o], o_out.at[c], sib)
    mine_out = local(outs.at[c], o_out.at[c])
    mine_out.wait()
    got(k_out, o_out.at[o], sib)
    finish_own()
    finish_cpy()
    for copy in sends:
        copy.wait_send()


def placing(assign, copy_share, copy_plan, experts):
    expert_of = assign[:, 0]
    numbers = jnp.arange(experts, dtype=jnp.int32)
    onehot = (expert_of[:, None] == numbers[None, :]).astype(jnp.int32)
    before = jnp.cumsum(onehot, axis=0) - onehot
    rank_in = jnp.sum(before * onehot, axis=1)
    limit_rows = jnp.sum(copy_share[0][None, :] * onehot, axis=1)
    holder = jnp.sum(
        numbers[None, :] * (copy_plan[None, :] == expert_of[:, None]).astype(jnp.int32), axis=1
    )
    core = lax.rem(lax.axis_index("dp"), 2)
    array = jnp.arange(2, dtype=jnp.int32)[:, None]
    spot = array * 4 + core * 2 + rank_in[None, :]
    owned = expert_of[None, :] * 16 + spot
    copied = jnp.where((rank_in < limit_rows)[None, :], holder[None, :] * 16 + 8 + spot, -1)
    places = jnp.arange(LANES, dtype=jnp.int32)
    hit = jnp.logical_or(places == owned[:, :, None], places == copied[:, :, None])
    return hit.astype(BF16).reshape(-1, LANES)


def body(tokens, assign, copy_share, copy_plan, grad_out, w_gate, w_up, w_down):
    rows_in, width = tokens.shape
    experts = lax.axis_size("expert")
    units = w_gate.shape[2]
    half = width // 2
    full = half + LANES
    chunk = half // 7
    part_p = 3 * chunk
    per_chip = 4 * experts
    slots = 8 * per_chip
    block = 2 * per_chip
    mid = block // 2
    marks = placing(assign, copy_share, copy_plan, experts)
    both = jnp.concatenate([tokens, grad_out], axis=0)
    ext = jnp.stack(
        [
            jnp.concatenate([both[:, :half], marks], axis=1),
            jnp.concatenate([both[:, half:], marks], axis=1),
        ]
    )
    vmem = pltpu.VMEM
    part_q = half - part_p
    messages = 128
    any_spec = pl.BlockSpec(memory_space=pl.ANY)
    o, g, u, d, cg, cu, cd = pl.pallas_call(
        functools.partial(kernel, experts, half, part_p, chunk),
        out_shape=[
            jax.ShapeDtypeStruct((2, 16, half), BF16),
            jax.ShapeDtypeStruct(w_gate.shape, BF16),
            jax.ShapeDtypeStruct(w_up.shape, BF16),
            jax.ShapeDtypeStruct(w_down.shape, BF16),
            jax.ShapeDtypeStruct(w_gate.shape, BF16),
            jax.ShapeDtypeStruct(w_up.shape, BF16),
            jax.ShapeDtypeStruct(w_down.shape, BF16),
        ],
        in_specs=[
            pl.BlockSpec(memory_space=pltpu.SMEM),
            pl.BlockSpec(memory_space=pltpu.VMEM),
            any_spec,
            any_spec,
            any_spec,
        ],
        out_specs=[any_spec] * 7,
        scratch_shapes=[
            vmem((2, 16, full), BF16),
            vmem((experts, 16, full), BF16),
            vmem((experts, 16, full), BF16),
            vmem((8, block, full), BF16),
            vmem((8, block, half), BF16),
            vmem((2, half, 2 * units), BF16),
            vmem((2 * units, half), BF16),
            vmem((2, slots, 3 * units), F32),
            vmem((slots, 3 * units), F32),
            vmem((2, slots, 3 * units), BF16),
            vmem((experts, slots // experts, 3 * units), BF16),
            vmem((experts, slots // experts, 3 * units), BF16),
            vmem((2, experts, slots // experts, 3 * units), BF16),
            vmem((slots, 4 * units), BF16),
            vmem((slots, 2 * units), BF16),
            vmem((8, block, half), BF16),
            vmem((4, block, part_p), BF16),
            vmem((2, mid, part_p), BF16),
            vmem((2, block, part_p), BF16),
            vmem((2, 2, mid, part_q), BF16),
            vmem((2, 2, block, part_q), BF16),
            vmem((block, part_q), BF16),
            vmem((block, half), BF16),
            vmem((experts, 16, half // 2), BF16),
            vmem((experts, 16, half // 2), BF16),
            vmem((2, 16, half), BF16),
            vmem((2, half, 2 * units), BF16),
            vmem((2 * units, half), BF16),
            vmem((2, half, 2 * units), BF16),
            vmem((2 * units, half), BF16),
            pltpu.SemaphoreType.DMA((messages,)),
            pltpu.SemaphoreType.DMA((messages,)),
            pltpu.SemaphoreType.DMA((16,)),
        ],
        compiler_params=pltpu.CompilerParams(
            collective_id=0,
            has_side_effects=True,
            vmem_limit_bytes=56 * 1024 * 1024,
        ),
        cost_estimate=pl.CostEstimate(
            flops=6_000_000_000, bytes_accessed=30_000_000, transcendentals=32768
        ),
    )(copy_plan, ext, w_gate, w_up, w_down)
    mixed = jnp.concatenate([o[0, :rows_in], o[1, :rows_in]], axis=1)
    grad_in = jnp.concatenate([o[0, rows_in:], o[1, rows_in:]], axis=1)
    return (mixed, grad_in, g, u, d, cg, cu, cd)


def solution(mesh):
    placed = (
        P(("dp", "expert"), None),
        P(("dp", "expert"), None),
        P(("dp", "expert"), None),
        P(),
        P(("dp", "expert"), None),
        P("expert", None, "dp"),
        P("expert", None, "dp"),
        P("expert", "dp", None),
    )
    return jax.shard_map(
        body,
        mesh=mesh,
        in_specs=placed,
        out_specs=(
            P(("dp", "expert"), None),
            P(("dp", "expert"), None),
            P("expert", None, "dp"),
            P("expert", None, "dp"),
            P("expert", "dp", None),
            P("expert", None, "dp"),
            P("expert", None, "dp"),
            P("expert", "dp", None),
        ),
        check_vma=False,
    )
```

```python
import functools

import jax
import jax.numpy as jnp
from jax import lax
from jax.experimental import pallas as pl
from jax.experimental.pallas import tpu as pltpu
from jax.sharding import PartitionSpec as P

MESH = pl.DeviceIdType.MESH
BF16 = jnp.bfloat16
F32 = jnp.float32
LANES = 128


def dot(a, b):
    return jnp.dot(a, b, preferred_element_type=F32)


def dot_nt(a, b):
    return lax.dot_general(a, b, (((1,), (1,)), ((), ())), preferred_element_type=F32)


def dot_tn(a, b):
    return lax.dot_general(a, b, (((0,), (0,)), ((), ())), preferred_element_type=F32)


def kernel(
    experts,
    half,
    part_p,
    chunk,
    plan_ref,
    assign_ref,
    share_ref,
    tok_ref,
    cot_ref,
    w_gate,
    w_up,
    w_down,
    o_out,
    gate_out,
    up_out,
    down_out,
    copy_gate_out,
    copy_up_out,
    copy_down_out,
    ext,
    raw,
    own_send,
    own_recv,
    cpy_send,
    cpy_recv,
    own,
    cpy,
    w1,
    wd,
    pre,
    pre_recv,
    acts,
    gx1,
    gx2s,
    gx2,
    gcat,
    hcat,
    part,
    rz,
    rxo,
    rxf,
    ro_q,
    rf_q,
    rzq,
    fin,
    back_send,
    back_recv,
    outs,
    st1,
    st2,
    ct1,
    ct2,
    ssem,
    rsem,
    lsem,
):
    units = w1.shape[2] // 2
    full = half + LANES
    per_chip = 4 * experts
    slots = 8 * per_chip
    block = 2 * per_chip
    mid = block // 2
    steps = half // chunk
    part_q = half - part_p

    dp = lax.axis_index("dp")
    ex = lax.axis_index("expert")
    x = dp // 4
    z = (dp // 2) % 2
    c = dp % 2
    o = 1 - c

    def chip(dx, zz):
        return lax.rem(x + dx, 4) * 2 + zz

    me = chip(0, z)
    xp = (lax.rem(dp + 4, 16), ex)
    xm = (lax.rem(dp + 12, 16), ex)
    zp = (dp + 2 - 4 * z, ex)
    sib = (dp + 1 - 2 * c, ex)

    def peer(i):
        return (dp, lax.rem(ex + i, experts))

    used = [0]
    sends = []

    def fresh():
        used[0] += 1
        return used[0] - 1

    def msg(k, src, dst, dev):
        copy = pltpu.make_async_remote_copy(
            src_ref=src,
            dst_ref=dst,
            send_sem=ssem.at[k],
            recv_sem=rsem.at[k],
            device_id=dev,
            device_id_type=MESH,
        )
        copy.start()
        sends.append(copy)

    def got(k, ref, dev):
        pltpu.make_async_remote_copy(
            src_ref=ref,
            dst_ref=ref,
            send_sem=ssem.at[k],
            recv_sem=rsem.at[k],
            device_id=dev,
            device_id_type=MESH,
        ).wait_recv()

    used_local = [0]

    def local(src, dst):
        copy = pltpu.make_async_copy(src, dst, lsem.at[used_local[0]])
        used_local[0] += 1
        copy.start()
        return copy

    my_rows = pl.ds(pl.multiple_of(c * half, half), half)
    other_rows = pl.ds(pl.multiple_of(o * half, half), half)

    weight_loads = [
        local(w_gate.at[0, my_rows, :], w1.at[0, :, pl.ds(0, units)]),
        local(w_up.at[0, my_rows, :], w1.at[0, :, pl.ds(units, units)]),
        local(w_down.at[0, :, my_rows], wd.at[pl.ds(0, units), :]),
    ]

    barrier = pltpu.get_barrier_semaphore()
    greeted = [xp, xm, zp, sib] + [peer(i) for i in range(1, experts)]
    for dev in greeted:
        pl.semaphore_signal(barrier, inc=1, device_id=dev, device_id_type=MESH)

    line = lax.broadcasted_iota(jnp.int32, (16, LANES), 0)
    owned = jnp.zeros((16, LANES), jnp.int32)
    copied = jnp.zeros((16, LANES), jnp.int32)
    named = [assign_ref[t] for t in range(8)]
    for t in range(8):
        rank = jnp.int32(0)
        for earlier in range(t):
            rank += (named[earlier] == named[t]).astype(jnp.int32)
        holder = jnp.int32(0)
        for i in range(1, experts):
            holder += i * (plan_ref[i] == named[t]).astype(jnp.int32)
        spot = c * 2 + rank
        aside = jnp.where(rank < share_ref[named[t]], holder * 16 + 8 + spot, -LANES)
        here = line % 8 == t
        owned = jnp.where(here, named[t] * 16 + spot, owned)
        copied = jnp.where(here, aside, copied)
    shift = (line // 8) * 4
    lane = lax.broadcasted_iota(jnp.int32, (16, LANES), 1)
    marks = jnp.logical_or(lane == owned + shift, lane == copied + shift).astype(F32).astype(BF16)

    def stack(cols):
        return jnp.concatenate(
            [tok_ref[:, cols].astype(F32), cot_ref[:, cols].astype(F32)], axis=0
        ).astype(BF16)

    ext[:, :half] = stack(other_rows)
    ext[:, half:] = marks
    raw[c, :, :half] = stack(my_rows)
    raw[c, :, half:] = marks
    pl.semaphore_wait(barrier, len(greeted))

    k_raw = fresh()
    msg(k_raw, ext, raw.at[c], sib)
    k_w = [fresh() for _ in range(3)]
    msg(k_w[0], w_gate.at[0, other_rows, :], w1.at[1, :, pl.ds(0, units)], sib)
    msg(k_w[1], w_up.at[0, other_rows, :], w1.at[1, :, pl.ds(units, units)], sib)
    msg(k_w[2], w_down.at[0, :, other_rows], wd.at[pl.ds(units, units), :], sib)
    got(k_raw, raw.at[o], sib)

    size = 16 * experts
    quarter = half // 2
    spots = raw[:, :, half:full].reshape(32, LANES)[:, :size].astype(F32)
    lane = lax.broadcasted_iota(jnp.int32, (32, size), 1)
    own_spots = jnp.where((lane // 8) % 2 == 0, spots, 0.0)
    cpy_spots = jnp.where((lane // 8) % 2 == 1, spots, 0.0)
    left = raw[:, :, :quarter].reshape(32, quarter)
    right = raw[:, :, quarter:half].reshape(32, quarter)
    own_left = own_spots.astype(BF16)
    own_right = pltpu.roll(own_spots, 8, 1).astype(BF16)
    cpy_left = pltpu.roll(cpy_spots, size - 8, 1).astype(BF16)
    cpy_right = cpy_spots.astype(BF16)

    def spread(buf, first, second):
        buf[:, :, :quarter] = (
            (dot_tn(first, left) + dot_tn(second, right)).astype(BF16).reshape(experts, 16, quarter)
        )

    spread(own_send, own_left, own_right)
    own_send[:, :, quarter:] = (
        dot_tn(own_left, raw[:, :, half:full].reshape(32, LANES))
        .astype(BF16)
        .reshape(experts, 16, LANES)
    )
    k_own = [fresh() for _ in range(experts - 1)]
    for i in range(1, experts):
        dev = peer(i)
        msg(k_own[i - 1], own_send.at[dev[1]], own_recv.at[ex], dev)
    own_recv[ex] = own_send[ex]
    spread(cpy_send, cpy_left, cpy_right)
    k_cpy = [fresh() for _ in range(experts - 1)]
    for i in range(1, experts):
        dev = peer(i)
        msg(k_cpy[i - 1], cpy_send.at[dev[1]], cpy_recv.at[ex], dev)
    cpy_recv[ex] = cpy_send[ex]

    to = lax.broadcasted_iota(jnp.int32, (block, size), 0)
    fr = lax.broadcasted_iota(jnp.int32, (block, size), 1)
    match = to == ((fr // 4) % 2) * per_chip + (fr // 16) * 4 + fr % 4
    take_left = jnp.logical_and(match, (fr // 8) % 2 == 0).astype(BF16)
    take_right = jnp.logical_and(match, (fr // 8) % 2 == 1).astype(BF16)

    for i in range(1, experts):
        got(k_own[i - 1], own_recv.at[lax.rem(ex + experts - i, experts)], peer(i))
    arrived = own_recv[...].reshape(size, quarter + LANES)
    own[me, :, :quarter] = dot(take_left, arrived[:, :quarter]).astype(BF16)
    own[me, :, quarter:half] = dot(take_right, arrived[:, :quarter]).astype(BF16)
    own[me, :, half:] = dot(take_left, arrived[:, quarter:]).astype(BF16)

    def gather(buf, width):
        keys = [fresh() for _ in range(18)]

        def cut(q, lane, row=None):
            start, count = (0, block) if row is None else (row * mid, mid)
            if lane == 0:
                return buf.at[q, pl.ds(start, count), pl.ds(0, part_p)]
            return buf.at[q, pl.ds(start, count), pl.ds(part_p, width - part_p)]

        y = 1 - z

        def first():
            msg(keys[9], cut(me, 1), cut(me, 1), zp)
            msg(keys[0], cut(me, 0), cut(me, 0), xp)
            msg(keys[1], cut(me, 0), cut(me, 0), xm)
            msg(keys[2], cut(me, 0), cut(me, 0), zp)
            msg(keys[10], cut(me, 1), cut(me, 1), xp)
            msg(keys[11], cut(me, 1), cut(me, 1), xm)

        def second():
            got(keys[9], cut(chip(0, y), 1), zp)
            msg(keys[12], cut(chip(0, y), 1), cut(chip(0, y), 1), xp)
            msg(keys[13], cut(chip(0, y), 1), cut(chip(0, y), 1), xm)
            got(keys[0], cut(chip(3, z), 0), xm)
            msg(keys[3], cut(chip(3, z), 0, 0), cut(chip(3, z), 0, 0), xp)
            msg(keys[5], cut(chip(3, z), 0), cut(chip(3, z), 0), zp)
            got(keys[1], cut(chip(1, z), 0), xp)
            msg(keys[4], cut(chip(1, z), 0, 1), cut(chip(1, z), 0, 1), xm)
            msg(keys[6], cut(chip(1, z), 0), cut(chip(1, z), 0), zp)

        def third():
            got(keys[10], cut(chip(3, z), 1), xm)
            msg(keys[14], cut(chip(3, z), 1, 0), cut(chip(3, z), 1, 0), xp)
            got(keys[11], cut(chip(1, z), 1), xp)
            msg(keys[15], cut(chip(1, z), 1, 1), cut(chip(1, z), 1, 1), xm)
            got(keys[3], cut(chip(2, z), 0, 0), xm)
            msg(keys[7], cut(chip(2, z), 0, 0), cut(chip(2, z), 0, 0), zp)
            got(keys[4], cut(chip(2, z), 0, 1), xp)
            msg(keys[8], cut(chip(2, z), 0, 1), cut(chip(2, z), 0, 1), zp)
            got(keys[12], cut(chip(3, y), 1), xm)
            msg(keys[16], cut(chip(3, y), 1, 0), cut(chip(3, y), 1, 0), xp)
            got(keys[13], cut(chip(1, y), 1), xp)
            msg(keys[17], cut(chip(1, y), 1, 1), cut(chip(1, y), 1, 1), xm)

        def last():
            got(keys[2], cut(chip(0, y), 0), zp)
            got(keys[5], cut(chip(3, y), 0), zp)
            got(keys[6], cut(chip(1, y), 0), zp)
            got(keys[14], cut(chip(2, z), 1, 0), xm)
            got(keys[15], cut(chip(2, z), 1, 1), xp)
            got(keys[7], cut(chip(2, y), 0, 0), zp)
            got(keys[8], cut(chip(2, y), 0, 1), zp)
            got(keys[16], cut(chip(2, y), 1, 0), xm)
            got(keys[17], cut(chip(2, y), 1, 1), xp)

        return first, second, third, last

    own_first, own_second, own_third, own_last = gather(own, full)
    cpy_first, cpy_second, cpy_third, cpy_last = gather(cpy, half)
    own_first()
    own_second()
    own_third()
    for i in range(1, experts):
        got(k_cpy[i - 1], cpy_recv.at[lax.rem(ex + experts - i, experts)], peer(i))
    arrived = cpy_recv[...].reshape(size, quarter)
    cpy[me, :, :quarter] = dot(take_left, arrived).astype(BF16)
    cpy[me, :, quarter:] = dot(take_right, arrived).astype(BF16)
    cpy_first()

    for load in weight_loads:
        load.wait()
    got(k_w[0], w1.at[1, :, pl.ds(0, units)], sib)
    got(k_w[1], w1.at[1, :, pl.ds(units, units)], sib)
    got(k_w[2], wd.at[pl.ds(units, units), :], sib)
    own_last()

    pre[...] = jnp.zeros_like(pre)

    def tokens_of(buf, cols):
        return buf[:, :per_chip, cols].reshape(slots, chunk)

    def backs_of(buf, cols):
        return buf[:, per_chip:, cols].reshape(slots, chunk)

    @pl.loop(0, steps)
    def _(step):
        cols = pl.ds(pl.multiple_of(step * chunk, chunk), chunk)
        t = tokens_of(own, cols)
        g = backs_of(own, cols)
        pre[0, :, : 2 * units] += dot(t, w1[0, cols, :])
        pre[1, :, : 2 * units] += dot(t, w1[1, cols, :])
        gh = dot_nt(g, wd[:, cols])
        pre[0, :, 2 * units :] += gh[:, :units]
        pre[1, :, 2 * units :] += gh[:, units:]

    k_pre = fresh()
    msg(k_pre, pre.at[1], pre_recv, sib)
    cpy_second()
    got(k_pre, pre_recv, sib)
    total = pre[0] + pre_recv[...]
    gate = total[:, :units]
    up = total[:, units : 2 * units]
    grad_hidden = total[:, 2 * units :]
    squash = jax.nn.sigmoid(gate)
    acts[0, :, :units] = (gate * squash * up).astype(BF16)
    acts[0, :, units : 2 * units] = (
        grad_hidden * up * squash * (1.0 + gate * (1.0 - squash))
    ).astype(BF16)
    acts[0, :, 2 * units :] = (grad_hidden * gate * squash).astype(BF16)
    k_acts = fresh()
    msg(k_acts, acts.at[0], acts.at[1], sib)

    k_gx1 = [fresh() for _ in range(experts - 1)]
    for i in range(1, experts):
        dev = peer(i)
        piece = pl.ds(pl.multiple_of(dev[1] * (slots // experts), slots // experts), slots // experts)
        msg(k_gx1[i - 1], acts.at[0, piece, :], gx1.at[ex], dev)
    piece = pl.ds(pl.multiple_of(ex * (slots // experts), slots // experts), slots // experts)
    gx1[ex] = acts[0, piece, :]

    got(k_acts, acts.at[1], sib)
    hcat[:, :units] = acts[0, :, :units]
    hcat[:, units:] = acts[1, :, :units]

    @pl.loop(0, steps)
    def _(step):
        cols = pl.ds(pl.multiple_of(step * chunk, chunk), chunk)
        m = dot(hcat[...], wd[:, cols])
        part[:, :per_chip, cols] = m.astype(BF16).reshape(8, per_chip, chunk)
        r = dot_nt(acts[0, :, units:], w1[0, cols, :]) + dot_nt(acts[1, :, units:], w1[1, cols, :])
        part[:, per_chip:, cols] = r.astype(BF16).reshape(8, per_chip, chunk)

    cols_p = pl.ds(0, part_p)
    cols_q = pl.ds(part_p, part_q)
    first_rows = pl.ds(0, mid)
    last_rows = pl.ds(mid, mid)
    every = pl.ds(0, block)
    y = 1 - z

    k_z = [fresh() for _ in range(4)]
    k_xo = [fresh() for _ in range(2)]
    k_xf = [fresh() for _ in range(2)]
    k_yo = [[fresh() for _ in range(2)] for _ in range(2)]
    k_yf = [[fresh() for _ in range(2)] for _ in range(2)]
    k_w0 = fresh()

    def add(ref, extra):
        ref[...] = (ref[...].astype(F32) + extra[...].astype(F32)).astype(BF16)

    for j in (2, 1, 3, 0):
        msg(k_z[j], part.at[chip(j, y), every, cols_p], rz.at[j], zp)
    for i, zz in enumerate((y, z)):
        msg(k_yo[i][0], part.at[chip(2, zz), first_rows, cols_q], ro_q.at[i, 0], xp)
        msg(k_yo[i][1], part.at[chip(2, zz), last_rows, cols_q], ro_q.at[i, 1], xm)
    cpy_third()

    for i in range(1, experts):
        got(k_gx1[i - 1], gx1.at[lax.rem(ex + experts - i, experts)], peer(i))
    for i in range(experts):
        gx2s[i] = gx1[plan_ref[i]]
    k_gx2 = [fresh() for _ in range(experts - 1)]
    for i in range(1, experts):
        dev = peer(i)
        msg(k_gx2[i - 1], gx2s.at[dev[1]], gx2.at[0, ex], dev)
    gx2[0, ex] = gx2s[ex]

    marks = own[:, :per_chip, half:full].reshape(slots, LANES).astype(F32)
    lane = lax.broadcasted_iota(jnp.int32, (slots, LANES), 1)
    copied = jnp.sum(jnp.where((lane // 8) % 2 == 1, marks, 0.0), axis=1, keepdims=True)
    kept = 1.0 - copied
    gcat[:, : 2 * units] = (acts[0, :, units:].astype(F32) * kept).astype(BF16)
    gcat[:, 2 * units :] = (acts[1, :, units:].astype(F32) * kept).astype(BF16)
    hcat[...] = (hcat[...].astype(F32) * kept).astype(BF16)

    def weight_grads(buf, one, two):
        @pl.loop(0, steps)
        def _(step):
            cols = pl.ds(pl.multiple_of(step * chunk, chunk), chunk)
            d = dot_tn(tokens_of(buf, cols), gcat[...]).astype(BF16)
            one[0, cols, :] = d[:, : 2 * units]
            one[1, cols, :] = d[:, 2 * units :]
            two[:, cols] = dot_tn(hcat[...], backs_of(buf, cols)).astype(BF16)

    def write_grads(one, two, g_out, u_out, d_out):
        keys = [fresh() for _ in range(3)]
        lanes_g, lanes_u = pl.ds(0, units), pl.ds(units, units)
        msg(keys[0], one.at[1, :, lanes_g], g_out.at[0, my_rows, :], sib)
        msg(keys[1], one.at[1, :, lanes_u], u_out.at[0, my_rows, :], sib)
        msg(keys[2], two.at[lanes_u, :], d_out.at[0, :, my_rows], sib)
        mine = [
            local(one.at[0, :, lanes_g], g_out.at[0, my_rows, :]),
            local(one.at[0, :, lanes_u], u_out.at[0, my_rows, :]),
            local(two.at[lanes_g, :], d_out.at[0, :, my_rows]),
        ]

        def finish():
            for copy in mine:
                copy.wait()
            got(keys[0], g_out.at[0, other_rows, :], sib)
            got(keys[1], u_out.at[0, other_rows, :], sib)
            got(keys[2], d_out.at[0, :, other_rows], sib)

        return finish

    weight_grads(own, st1, st2)
    finish_own = write_grads(st1, st2, gate_out, up_out, down_out)

    for i, zz in enumerate((y, z)):
        got(k_yo[i][0], ro_q.at[i, 0], xm)
        add(part.at[chip(1, zz), first_rows, cols_q], ro_q.at[i, 0])
        msg(k_yf[i][0], part.at[chip(1, zz), every, cols_q], rf_q.at[i, 0], xp)
        got(k_yo[i][1], ro_q.at[i, 1], xp)
        add(part.at[chip(3, zz), last_rows, cols_q], ro_q.at[i, 1])
        msg(k_yf[i][1], part.at[chip(3, zz), every, cols_q], rf_q.at[i, 1], xm)
    got(k_z[2], rz.at[2], zp)
    add(part.at[chip(2, z), every, cols_p], rz.at[2])
    msg(k_xo[0], part.at[chip(2, z), first_rows, cols_p], rxo.at[0], xp)
    msg(k_xo[1], part.at[chip(2, z), last_rows, cols_p], rxo.at[1], xm)
    got(k_z[1], rz.at[1], zp)
    add(part.at[chip(1, z), every, cols_p], rz.at[1])
    got(k_z[3], rz.at[3], zp)
    add(part.at[chip(3, z), every, cols_p], rz.at[3])
    got(k_xo[0], rxo.at[0], xm)
    add(part.at[chip(1, z), first_rows, cols_p], rxo.at[0])
    msg(k_xf[0], part.at[chip(1, z), every, cols_p], rxf.at[0], xp)
    got(k_xo[1], rxo.at[1], xp)
    add(part.at[chip(3, z), last_rows, cols_p], rxo.at[1])
    msg(k_xf[1], part.at[chip(3, z), every, cols_p], rxf.at[1], xm)

    got(k_yf[0][0], rf_q.at[0, 0], xm)
    got(k_yf[0][1], rf_q.at[0, 1], xp)
    mine_y = part.at[chip(0, y), every, cols_q]
    mine_y[...] = (
        mine_y[...].astype(F32) + rf_q[0, 0].astype(F32) + rf_q[0, 1].astype(F32)
    ).astype(BF16)
    msg(k_w0, mine_y, rzq, zp)

    cpy_last()
    for i in range(1, experts):
        got(k_gx2[i - 1], gx2.at[0, lax.rem(ex + experts - i, experts)], peer(i))
    k_gsib = fresh()
    msg(k_gsib, gx2.at[0], gx2.at[1], sib)

    got(k_gsib, gx2.at[1], sib)
    for i in range(2):
        gcat[:, 2 * units * i : 2 * units * (i + 1)] = gx2[i, :, :, units:].reshape(
            slots, 2 * units
        )
        hcat[:, units * i : units * (i + 1)] = gx2[i, :, :, :units].reshape(slots, units)
    weight_grads(cpy, ct1, ct2)
    finish_cpy = write_grads(ct1, ct2, copy_gate_out, copy_up_out, copy_down_out)

    got(k_z[0], rz.at[0], zp)
    got(k_xf[0], rxf.at[0], xm)
    got(k_xf[1], rxf.at[1], xp)
    fin[:, cols_p] = (
        part[me, :, cols_p].astype(F32)
        + rz[0].astype(F32)
        + rxf[0].astype(F32)
        + rxf[1].astype(F32)
    ).astype(BF16)
    got(k_yf[1][0], rf_q.at[1, 0], xm)
    got(k_yf[1][1], rf_q.at[1, 1], xp)
    got(k_w0, rzq, zp)
    fin[:, cols_q] = (
        part[me, :, cols_q].astype(F32)
        + rf_q[1, 0].astype(F32)
        + rf_q[1, 1].astype(F32)
        + rzq[...].astype(F32)
    ).astype(BF16)

    to = lax.broadcasted_iota(jnp.int32, (size, block), 0)
    fr = lax.broadcasted_iota(jnp.int32, (size, block), 1)
    want = (to // 16) * 4 + ((to // 4) % 2) * per_chip + to % 4
    side = (to // 8) % 2
    back_send[...] = (
        dot(jnp.logical_and(fr == want, side == 0).astype(BF16), fin[:, :quarter])
        + dot(jnp.logical_and(fr == want, side == 1).astype(BF16), fin[:, quarter:])
    ).astype(BF16).reshape(experts, 16, quarter)
    k_back = [fresh() for _ in range(experts - 1)]
    for i in range(1, experts):
        dev = peer(i)
        msg(k_back[i - 1], back_send.at[dev[1]], back_recv.at[ex], dev)
    back_recv[ex] = back_send[ex]

    for i in range(1, experts):
        got(k_back[i - 1], back_recv.at[lax.rem(ex + experts - i, experts)], peer(i))
    got_back = back_recv[...].reshape(size, quarter)
    outs[:, :, :quarter] = dot(own_left, got_back).astype(BF16).reshape(2, 16, quarter)
    outs[:, :, quarter:] = dot(own_right, got_back).astype(BF16).reshape(2, 16, quarter)
    k_out = fresh()
    msg(k_out, outs.at[o], o_out.at[c], sib)
    mine_out = local(outs.at[c], o_out.at[c])
    mine_out.wait()
    got(k_out, o_out.at[o], sib)
    finish_own()
    finish_cpy()
    for copy in sends:
        copy.wait_send()


def finish(o, g, u, d, cg, cu, cd, mixed, grad_in, g_out, u_out, d_out, cg_out, cu_out, cd_out, sem):
    copies = []
    pairs = ((g, g_out), (u, u_out), (d, d_out), (cg, cg_out), (cu, cu_out), (cd, cd_out))
    for i, (src, dst) in enumerate(pairs):
        copies.append(pltpu.make_async_copy(src, dst, sem.at[i]))
        copies[-1].start()
    half = o.shape[2]
    for side in range(2):
        mixed[:, half * side : half * (side + 1)] = o[side, :8, :]
        grad_in[:, half * side : half * (side + 1)] = o[side, 8:, :]
    for copy in copies:
        copy.wait()


def body(tokens, assign, copy_share, copy_plan, grad_out, w_gate, w_up, w_down):
    rows_in, width = tokens.shape
    experts = lax.axis_size("expert")
    units = w_gate.shape[2]
    half = width // 2
    full = half + LANES
    chunk = half // 7
    part_p = 3 * chunk
    per_chip = 4 * experts
    slots = 8 * per_chip
    block = 2 * per_chip
    mid = block // 2
    vmem = pltpu.VMEM
    part_q = half - part_p
    messages = 128
    any_spec = pl.BlockSpec(memory_space=pl.ANY)
    smem_spec = pl.BlockSpec(memory_space=pltpu.SMEM)
    vmem_spec = pl.BlockSpec(memory_space=pltpu.VMEM)
    o, g, u, d, cg, cu, cd = pl.pallas_call(
        functools.partial(kernel, experts, half, part_p, chunk),
        out_shape=[
            jax.ShapeDtypeStruct((2, 16, half), BF16),
            jax.ShapeDtypeStruct(w_gate.shape, BF16),
            jax.ShapeDtypeStruct(w_up.shape, BF16),
            jax.ShapeDtypeStruct(w_down.shape, BF16),
            jax.ShapeDtypeStruct(w_gate.shape, BF16),
            jax.ShapeDtypeStruct(w_up.shape, BF16),
            jax.ShapeDtypeStruct(w_down.shape, BF16),
        ],
        in_specs=[
            smem_spec,
            smem_spec,
            smem_spec,
            vmem_spec,
            vmem_spec,
            any_spec,
            any_spec,
            any_spec,
        ],
        out_specs=[any_spec] * 7,
        scratch_shapes=[
            vmem((16, full), BF16),
            vmem((2, 16, full), BF16),
            vmem((experts, 16, half // 2 + LANES), BF16),
            vmem((experts, 16, half // 2 + LANES), BF16),
            vmem((experts, 16, half // 2), BF16),
            vmem((experts, 16, half // 2), BF16),
            vmem((8, block, full), BF16),
            vmem((8, block, half), BF16),
            vmem((2, half, 2 * units), BF16),
            vmem((2 * units, half), BF16),
            vmem((2, slots, 3 * units), F32),
            vmem((slots, 3 * units), F32),
            vmem((2, slots, 3 * units), BF16),
            vmem((experts, slots // experts, 3 * units), BF16),
            vmem((experts, slots // experts, 3 * units), BF16),
            vmem((2, experts, slots // experts, 3 * units), BF16),
            vmem((slots, 4 * units), BF16),
            vmem((slots, 2 * units), BF16),
            vmem((8, block, half), BF16),
            vmem((4, block, part_p), BF16),
            vmem((2, mid, part_p), BF16),
            vmem((2, block, part_p), BF16),
            vmem((2, 2, mid, part_q), BF16),
            vmem((2, 2, block, part_q), BF16),
            vmem((block, part_q), BF16),
            vmem((block, half), BF16),
            vmem((experts, 16, half // 2), BF16),
            vmem((experts, 16, half // 2), BF16),
            vmem((2, 16, half), BF16),
            vmem((2, half, 2 * units), BF16),
            vmem((2 * units, half), BF16),
            vmem((2, half, 2 * units), BF16),
            vmem((2 * units, half), BF16),
            pltpu.SemaphoreType.DMA((messages,)),
            pltpu.SemaphoreType.DMA((messages,)),
            pltpu.SemaphoreType.DMA((16,)),
        ],
        compiler_params=pltpu.CompilerParams(
            collective_id=0,
            has_side_effects=True,
            vmem_limit_bytes=42 * 1024 * 1024,
        ),
        cost_estimate=pl.CostEstimate(
            flops=6_000_000_000, bytes_accessed=30_000_000, transcendentals=32768
        ),
    )(
        copy_plan,
        assign.reshape(rows_in),
        copy_share.reshape(experts),
        tokens,
        grad_out,
        w_gate,
        w_up,
        w_down,
    )
    return pl.pallas_call(
        finish,
        out_shape=[
            jax.ShapeDtypeStruct(tokens.shape, BF16),
            jax.ShapeDtypeStruct(tokens.shape, BF16),
            jax.ShapeDtypeStruct(w_gate.shape, BF16),
            jax.ShapeDtypeStruct(w_up.shape, BF16),
            jax.ShapeDtypeStruct(w_down.shape, BF16),
            jax.ShapeDtypeStruct(w_gate.shape, BF16),
            jax.ShapeDtypeStruct(w_up.shape, BF16),
            jax.ShapeDtypeStruct(w_down.shape, BF16),
        ],
        in_specs=[vmem_spec] + [any_spec] * 6,
        out_specs=[vmem_spec] * 2 + [any_spec] * 6,
        scratch_shapes=[pltpu.SemaphoreType.DMA((6,))],
        compiler_params=pltpu.CompilerParams(vmem_limit_bytes=4 * 1024 * 1024),
    )(o, g, u, d, cg, cu, cd)


def solution(mesh):
    placed = (
        P(("dp", "expert"), None),
        P(("dp", "expert"), None),
        P(("dp", "expert"), None),
        P(),
        P(("dp", "expert"), None),
        P("expert", None, "dp"),
        P("expert", None, "dp"),
        P("expert", "dp", None),
    )
    return jax.shard_map(
        body,
        mesh=mesh,
        in_specs=placed,
        out_specs=(
            P(("dp", "expert"), None),
            P(("dp", "expert"), None),
            P("expert", None, "dp"),
            P("expert", None, "dp"),
            P("expert", "dp", None),
            P("expert", None, "dp"),
            P("expert", None, "dp"),
            P("expert", "dp", None),
        ),
        check_vma=False,
    )
```

```python
import functools

import jax
import jax.numpy as jnp
from jax import lax
from jax.experimental import pallas as pl
from jax.experimental.pallas import tpu as pltpu
from jax.sharding import PartitionSpec as P

MESH = pl.DeviceIdType.MESH
BF16 = jnp.bfloat16
F32 = jnp.float32
LANES = 128


def dot(a, b):
    return jnp.dot(a, b, preferred_element_type=F32)


def dot_nt(a, b):
    return lax.dot_general(a, b, (((1,), (1,)), ((), ())), preferred_element_type=F32)


def dot_tn(a, b):
    return lax.dot_general(a, b, (((0,), (0,)), ((), ())), preferred_element_type=F32)


def kernel(
    experts,
    half,
    part_p,
    sum_p,
    chunk,
    ints_in,
    tok_in,
    cot_in,
    w_gate,
    w_up,
    w_down,
    o_out,
    gate_out,
    up_out,
    down_out,
    copy_gate_out,
    copy_up_out,
    copy_down_out,
    ints,
    tok_ref,
    cot_ref,
    ext,
    raw,
    own_send_p,
    own_recv_p,
    own_send_q,
    own_recv_q,
    cpy_send,
    cpy_recv,
    own,
    cpy,
    w1,
    wd,
    pre,
    pre_recv,
    acts,
    gx1,
    gx2s,
    gx2,
    gcat,
    hcat,
    part,
    rz,
    rxo,
    rxf,
    ro_q,
    rf_q,
    rzq,
    fin,
    back_send_p,
    back_recv_p,
    back_send_q,
    back_recv_q,
    outs,
    st1,
    st2,
    ct1,
    ct2,
    ssem,
    rsem,
    lsem,
):
    units = w1.shape[2] // 2
    full = half + LANES
    per_chip = 4 * experts
    slots = 8 * per_chip
    block = 2 * per_chip
    mid = block // 2
    steps = half // chunk
    sum_q = half - sum_p

    dp = lax.axis_index("dp")
    ex = lax.axis_index("expert")
    x = dp // 4
    z = (dp // 2) % 2
    c = dp % 2
    o = 1 - c

    def chip(dx, zz):
        return lax.rem(x + dx, 4) * 2 + zz

    me = chip(0, z)
    xp = (lax.rem(dp + 4, 16), ex)
    xm = (lax.rem(dp + 12, 16), ex)
    zp = (dp + 2 - 4 * z, ex)
    sib = (dp + 1 - 2 * c, ex)

    def peer(i):
        return (dp, lax.rem(ex + i, experts))

    used = [0]
    sends = []

    def fresh():
        used[0] += 1
        return used[0] - 1

    def msg(k, src, dst, dev):
        copy = pltpu.make_async_remote_copy(
            src_ref=src,
            dst_ref=dst,
            send_sem=ssem.at[k],
            recv_sem=rsem.at[k],
            device_id=dev,
            device_id_type=MESH,
        )
        copy.start()
        sends.append(copy)

    def got(k, ref, dev):
        pltpu.make_async_remote_copy(
            src_ref=ref,
            dst_ref=ref,
            send_sem=ssem.at[k],
            recv_sem=rsem.at[k],
            device_id=dev,
            device_id_type=MESH,
        ).wait_recv()

    used_local = [0]

    def local(src, dst):
        copy = pltpu.make_async_copy(src, dst, lsem.at[used_local[0]])
        used_local[0] += 1
        copy.start()
        return copy

    my_rows = pl.ds(pl.multiple_of(c * half, half), half)
    other_rows = pl.ds(pl.multiple_of(o * half, half), half)

    first_loads = [
        local(ints_in, ints),
        local(tok_in, tok_ref),
        local(cot_in, cot_ref),
    ]

    barrier = pltpu.get_barrier_semaphore()
    greeted = [xp, xm, zp, sib] + [peer(i) for i in range(1, experts)]
    for dev in greeted:
        pl.semaphore_signal(barrier, inc=1, device_id=dev, device_id_type=MESH)

    weight_loads = [
        local(w_gate.at[0, my_rows, :], w1.at[0, :, pl.ds(0, units)]),
        local(w_up.at[0, my_rows, :], w1.at[0, :, pl.ds(units, units)]),
        local(w_down.at[0, :, my_rows], wd.at[pl.ds(0, units), :]),
    ]

    for load in first_loads:
        load.wait()

    line = lax.broadcasted_iota(jnp.int32, (16, LANES), 0)
    owned = jnp.zeros((16, LANES), jnp.int32)
    copied = jnp.zeros((16, LANES), jnp.int32)
    named = [ints[experts + t] for t in range(8)]
    for t in range(8):
        rank = jnp.int32(0)
        for earlier in range(t):
            rank += (named[earlier] == named[t]).astype(jnp.int32)
        holder = jnp.int32(0)
        for i in range(1, experts):
            holder += i * (ints[i] == named[t]).astype(jnp.int32)
        spot = c * 2 + rank
        aside = jnp.where(rank < ints[experts + 8 + named[t]], holder * 16 + 8 + spot, -LANES)
        here = line % 8 == t
        owned = jnp.where(here, named[t] * 16 + spot, owned)
        copied = jnp.where(here, aside, copied)
    shift = (line // 8) * 4
    lane = lax.broadcasted_iota(jnp.int32, (16, LANES), 1)
    marks = jnp.logical_or(lane == owned + shift, lane == copied + shift).astype(F32).astype(BF16)

    def stack(cols):
        return jnp.concatenate(
            [tok_ref[:, cols].astype(F32), cot_ref[:, cols].astype(F32)], axis=0
        ).astype(BF16)

    ext[:, :half] = stack(other_rows)
    ext[:, half:] = marks
    raw[c, :, :half] = stack(my_rows)
    raw[c, :, half:] = marks
    pl.semaphore_wait(barrier, len(greeted))

    k_raw = fresh()
    msg(k_raw, ext, raw.at[c], sib)
    k_w = [fresh() for _ in range(3)]
    msg(k_w[0], w_gate.at[0, other_rows, :], w1.at[1, :, pl.ds(0, units)], sib)
    msg(k_w[1], w_up.at[0, other_rows, :], w1.at[1, :, pl.ds(units, units)], sib)
    msg(k_w[2], w_down.at[0, :, other_rows], wd.at[pl.ds(units, units), :], sib)
    got(k_raw, raw.at[o], sib)

    size = 16 * experts
    spots = raw[:, :, half:full].reshape(32, LANES)[:, :size].astype(F32)
    lane = lax.broadcasted_iota(jnp.int32, (32, size), 1)
    own_spots = jnp.where((lane // 8) % 2 == 0, spots, 0.0)
    cpy_spots = jnp.where((lane // 8) % 2 == 1, spots, 0.0)
    own_left = own_spots.astype(BF16)
    own_right = pltpu.roll(own_spots, 8, 1).astype(BF16)
    cpy_left = pltpu.roll(cpy_spots, size - 8, 1).astype(BF16)
    cpy_right = cpy_spots.astype(BF16)

    def spread(first, second, start, count):
        middle = start + count // 2
        left = raw[:, :, start:middle].reshape(32, count // 2)
        right = raw[:, :, middle : start + count].reshape(32, count // 2)
        both = dot_tn(first, left) + dot_tn(second, right)
        return both.astype(BF16).reshape(experts, 16, count // 2)

    def exchange(source, target):
        keys = [fresh() for _ in range(experts - 1)]
        for i in range(1, experts):
            dev = peer(i)
            msg(keys[i - 1], source.at[dev[1]], target.at[ex], dev)
        target[ex] = source[ex]

        def arrive():
            for i in range(1, experts):
                got(keys[i - 1], target.at[lax.rem(ex + experts - i, experts)], peer(i))

        return arrive

    side_q = (half - part_p) // 2
    own_send_p[...] = spread(own_left, own_right, 0, part_p)
    arrive_p = exchange(own_send_p, own_recv_p)
    own_send_q[:, :, :side_q] = spread(own_left, own_right, part_p, half - part_p)
    own_send_q[:, :, side_q:] = (
        dot_tn(own_left, raw[:, :, half:full].reshape(32, LANES))
        .astype(BF16)
        .reshape(experts, 16, LANES)
    )
    arrive_q = exchange(own_send_q, own_recv_q)
    cpy_send[...] = spread(cpy_left, cpy_right, 0, half)
    arrive_cpy = exchange(cpy_send, cpy_recv)

    to = lax.broadcasted_iota(jnp.int32, (block, size), 0)
    fr = lax.broadcasted_iota(jnp.int32, (block, size), 1)
    match = to == ((fr // 4) % 2) * per_chip + (fr // 16) * 4 + fr % 4
    take_left = jnp.logical_and(match, (fr // 8) % 2 == 0).astype(BF16)
    take_right = jnp.logical_and(match, (fr // 8) % 2 == 1).astype(BF16)

    def collect(buf, arrived, start, count):
        middle = start + count // 2
        rows = arrived[:, :, : count // 2].reshape(size, count // 2)
        buf[me, :, start:middle] = dot(take_left, rows).astype(BF16)
        buf[me, :, middle : start + count] = dot(take_right, rows).astype(BF16)

    def gather(buf, width):
        keys = [fresh() for _ in range(18)]

        def cut(q, lane, row=None):
            start, count = (0, block) if row is None else (row * mid, mid)
            if lane == 0:
                return buf.at[q, pl.ds(start, count), pl.ds(0, part_p)]
            return buf.at[q, pl.ds(start, count), pl.ds(part_p, width - part_p)]

        y = 1 - z

        def first_p():
            msg(keys[0], cut(me, 0), cut(me, 0), xp)
            msg(keys[1], cut(me, 0), cut(me, 0), xm)

        def first_q():
            msg(keys[9], cut(me, 1), cut(me, 1), zp)
            msg(keys[10], cut(me, 1), cut(me, 1), xp)
            msg(keys[11], cut(me, 1), cut(me, 1), xm)

        def second():
            got(keys[0], cut(chip(3, z), 0), xm)
            msg(keys[3], cut(chip(3, z), 0, 0), cut(chip(3, z), 0, 0), xp)
            msg(keys[5], cut(chip(3, z), 0), cut(chip(3, z), 0), zp)
            got(keys[1], cut(chip(1, z), 0), xp)
            msg(keys[4], cut(chip(1, z), 0, 1), cut(chip(1, z), 0, 1), xm)
            msg(keys[6], cut(chip(1, z), 0), cut(chip(1, z), 0), zp)
            got(keys[9], cut(chip(0, y), 1), zp)
            msg(keys[12], cut(chip(0, y), 1), cut(chip(0, y), 1), xp)
            msg(keys[13], cut(chip(0, y), 1), cut(chip(0, y), 1), xm)
            msg(keys[2], cut(me, 0), cut(me, 0), zp)

        def third():
            got(keys[10], cut(chip(3, z), 1), xm)
            msg(keys[14], cut(chip(3, z), 1, 0), cut(chip(3, z), 1, 0), xp)
            got(keys[11], cut(chip(1, z), 1), xp)
            msg(keys[15], cut(chip(1, z), 1, 1), cut(chip(1, z), 1, 1), xm)
            got(keys[3], cut(chip(2, z), 0, 0), xm)
            msg(keys[7], cut(chip(2, z), 0, 0), cut(chip(2, z), 0, 0), zp)
            got(keys[4], cut(chip(2, z), 0, 1), xp)
            msg(keys[8], cut(chip(2, z), 0, 1), cut(chip(2, z), 0, 1), zp)
            got(keys[12], cut(chip(3, y), 1), xm)
            msg(keys[16], cut(chip(3, y), 1, 0), cut(chip(3, y), 1, 0), xp)
            got(keys[13], cut(chip(1, y), 1), xp)
            msg(keys[17], cut(chip(1, y), 1, 1), cut(chip(1, y), 1, 1), xm)

        def last():
            got(keys[2], cut(chip(0, y), 0), zp)
            got(keys[5], cut(chip(3, y), 0), zp)
            got(keys[6], cut(chip(1, y), 0), zp)
            got(keys[14], cut(chip(2, z), 1, 0), xm)
            got(keys[15], cut(chip(2, z), 1, 1), xp)
            got(keys[7], cut(chip(2, y), 0, 0), zp)
            got(keys[8], cut(chip(2, y), 0, 1), zp)
            got(keys[16], cut(chip(2, y), 1, 0), xm)
            got(keys[17], cut(chip(2, y), 1, 1), xp)

        return first_p, first_q, second, third, last

    own_first_p, own_first_q, own_second, own_third, own_last = gather(own, full)
    cpy_first_p, cpy_first_q, cpy_second, cpy_third, cpy_last = gather(cpy, half)
    arrive_p()
    collect(own, own_recv_p, 0, part_p)
    own_first_p()
    arrive_q()
    collect(own, own_recv_q, part_p, half - part_p)
    own[me, :, half:] = dot(take_left, own_recv_q[:, :, side_q:].reshape(size, LANES)).astype(BF16)
    own_first_q()
    own_second()
    own_third()
    arrive_cpy()
    collect(cpy, cpy_recv, 0, half)
    cpy_first_p()
    cpy_first_q()

    for load in weight_loads:
        load.wait()
    got(k_w[0], w1.at[1, :, pl.ds(0, units)], sib)
    got(k_w[1], w1.at[1, :, pl.ds(units, units)], sib)
    got(k_w[2], wd.at[pl.ds(units, units), :], sib)
    own_last()

    def tokens_of(buf, cols):
        return buf[:, :per_chip, cols].reshape(slots, -1)

    def backs_of(buf, cols):
        return buf[:, per_chip:, cols].reshape(slots, -1)

    pre[1, :, : 2 * units] = dot(tokens_of(own, slice(0, half)), w1[1])
    gh = dot_nt(backs_of(own, slice(0, half)), wd[...])
    pre[1, :, 2 * units :] = gh[:, units:]
    k_pre = fresh()
    msg(k_pre, pre.at[1], pre_recv, sib)
    pre[0, :, : 2 * units] = dot(tokens_of(own, slice(0, half)), w1[0])
    pre[0, :, 2 * units :] = gh[:, :units]
    cpy_second()
    got(k_pre, pre_recv, sib)
    total = pre[0] + pre_recv[...]
    gate = total[:, :units]
    up = total[:, units : 2 * units]
    grad_hidden = total[:, 2 * units :]
    squash = jax.nn.sigmoid(gate)
    acts[0, :, :units] = (gate * squash * up).astype(BF16)
    acts[0, :, units : 2 * units] = (
        grad_hidden * up * squash * (1.0 + gate * (1.0 - squash))
    ).astype(BF16)
    acts[0, :, 2 * units :] = (grad_hidden * gate * squash).astype(BF16)
    k_acts = fresh()
    msg(k_acts, acts.at[0], acts.at[1], sib)

    k_gx1 = [fresh() for _ in range(experts - 1)]
    for i in range(1, experts):
        dev = peer(i)
        piece = pl.ds(pl.multiple_of(dev[1] * (slots // experts), slots // experts), slots // experts)
        msg(k_gx1[i - 1], acts.at[0, piece, :], gx1.at[ex], dev)
    piece = pl.ds(pl.multiple_of(ex * (slots // experts), slots // experts), slots // experts)
    gx1[ex] = acts[0, piece, :]

    got(k_acts, acts.at[1], sib)
    hcat[:, :units] = acts[0, :, :units]
    hcat[:, units:] = acts[1, :, :units]

    @pl.loop(0, steps)
    def _(step):
        cols = pl.ds(pl.multiple_of(step * chunk, chunk), chunk)
        m = dot(hcat[...], wd[:, cols])
        part[:, :per_chip, cols] = m.astype(BF16).reshape(8, per_chip, chunk)
        r = dot_nt(acts[0, :, units:], w1[0, cols, :]) + dot_nt(acts[1, :, units:], w1[1, cols, :])
        part[:, per_chip:, cols] = r.astype(BF16).reshape(8, per_chip, chunk)

    cols_p = pl.ds(0, sum_p)
    cols_q = pl.ds(sum_p, sum_q)
    first_rows = pl.ds(0, mid)
    last_rows = pl.ds(mid, mid)
    every = pl.ds(0, block)
    y = 1 - z

    k_z = [fresh() for _ in range(4)]
    k_xo = [fresh() for _ in range(2)]
    k_xf = [fresh() for _ in range(2)]
    k_yo = [[fresh() for _ in range(2)] for _ in range(2)]
    k_yf = [[fresh() for _ in range(2)] for _ in range(2)]
    k_w0 = fresh()

    def add(ref, extra):
        ref[...] = (ref[...].astype(F32) + extra[...].astype(F32)).astype(BF16)

    for j in (2, 1, 3, 0):
        msg(k_z[j], part.at[chip(j, y), every, cols_p], rz.at[j], zp)
    for i, zz in enumerate((y, z)):
        msg(k_yo[i][0], part.at[chip(2, zz), first_rows, cols_q], ro_q.at[i, 0], xp)
        msg(k_yo[i][1], part.at[chip(2, zz), last_rows, cols_q], ro_q.at[i, 1], xm)
    cpy_third()

    for i in range(1, experts):
        got(k_gx1[i - 1], gx1.at[lax.rem(ex + experts - i, experts)], peer(i))
    for i in range(experts):
        gx2s[i] = gx1[ints[i]]
    k_gx2 = [fresh() for _ in range(experts - 1)]
    for i in range(1, experts):
        dev = peer(i)
        msg(k_gx2[i - 1], gx2s.at[dev[1]], gx2.at[0, ex], dev)
    gx2[0, ex] = gx2s[ex]

    marks = own[:, :per_chip, half:full].reshape(slots, LANES).astype(F32)
    lane = lax.broadcasted_iota(jnp.int32, (slots, LANES), 1)
    copied = jnp.sum(jnp.where((lane // 8) % 2 == 1, marks, 0.0), axis=1, keepdims=True)
    kept = 1.0 - copied
    gcat[:, : 2 * units] = (acts[0, :, units:].astype(F32) * kept).astype(BF16)
    gcat[:, 2 * units :] = (acts[1, :, units:].astype(F32) * kept).astype(BF16)
    hcat[...] = (hcat[...].astype(F32) * kept).astype(BF16)

    def weight_grads(buf, one, two):
        @pl.loop(0, steps)
        def _(step):
            cols = pl.ds(pl.multiple_of(step * chunk, chunk), chunk)
            d = dot_tn(tokens_of(buf, cols), gcat[...]).astype(BF16)
            one[0, cols, :] = d[:, : 2 * units]
            one[1, cols, :] = d[:, 2 * units :]
            two[:, cols] = dot_tn(hcat[...], backs_of(buf, cols)).astype(BF16)

    def write_grads(one, two, g_out, u_out, d_out):
        keys = [fresh() for _ in range(3)]
        lanes_g, lanes_u = pl.ds(0, units), pl.ds(units, units)
        msg(keys[0], one.at[1, :, lanes_g], g_out.at[0, my_rows, :], sib)
        msg(keys[1], one.at[1, :, lanes_u], u_out.at[0, my_rows, :], sib)
        msg(keys[2], two.at[lanes_u, :], d_out.at[0, :, my_rows], sib)
        mine = [
            local(one.at[0, :, lanes_g], g_out.at[0, my_rows, :]),
            local(one.at[0, :, lanes_u], u_out.at[0, my_rows, :]),
            local(two.at[lanes_g, :], d_out.at[0, :, my_rows]),
        ]

        def finish():
            for copy in mine:
                copy.wait()
            got(keys[0], g_out.at[0, other_rows, :], sib)
            got(keys[1], u_out.at[0, other_rows, :], sib)
            got(keys[2], d_out.at[0, :, other_rows], sib)

        return finish

    weight_grads(own, st1, st2)
    finish_own = write_grads(st1, st2, gate_out, up_out, down_out)

    def pass_on(i, zz):
        got(k_yo[i][0], ro_q.at[i, 0], xm)
        add(part.at[chip(1, zz), first_rows, cols_q], ro_q.at[i, 0])
        msg(k_yf[i][0], part.at[chip(1, zz), every, cols_q], rf_q.at[i, 0], xp)
        got(k_yo[i][1], ro_q.at[i, 1], xp)
        add(part.at[chip(3, zz), last_rows, cols_q], ro_q.at[i, 1])
        msg(k_yf[i][1], part.at[chip(3, zz), every, cols_q], rf_q.at[i, 1], xm)

    pass_on(0, y)
    got(k_z[2], rz.at[2], zp)
    add(part.at[chip(2, z), every, cols_p], rz.at[2])
    msg(k_xo[0], part.at[chip(2, z), first_rows, cols_p], rxo.at[0], xp)
    msg(k_xo[1], part.at[chip(2, z), last_rows, cols_p], rxo.at[1], xm)
    got(k_z[1], rz.at[1], zp)
    add(part.at[chip(1, z), every, cols_p], rz.at[1])
    got(k_z[3], rz.at[3], zp)
    add(part.at[chip(3, z), every, cols_p], rz.at[3])
    pass_on(1, z)
    got(k_xo[0], rxo.at[0], xm)
    add(part.at[chip(1, z), first_rows, cols_p], rxo.at[0])
    msg(k_xf[0], part.at[chip(1, z), every, cols_p], rxf.at[0], xp)
    got(k_xo[1], rxo.at[1], xp)
    add(part.at[chip(3, z), last_rows, cols_p], rxo.at[1])
    msg(k_xf[1], part.at[chip(3, z), every, cols_p], rxf.at[1], xm)

    got(k_yf[0][0], rf_q.at[0, 0], xm)
    got(k_yf[0][1], rf_q.at[0, 1], xp)
    mine_y = part.at[chip(0, y), every, cols_q]
    mine_y[...] = (
        mine_y[...].astype(F32) + rf_q[0, 0].astype(F32) + rf_q[0, 1].astype(F32)
    ).astype(BF16)
    msg(k_w0, mine_y, rzq, zp)

    cpy_last()
    for i in range(1, experts):
        got(k_gx2[i - 1], gx2.at[0, lax.rem(ex + experts - i, experts)], peer(i))
    k_gsib = fresh()
    msg(k_gsib, gx2.at[0], gx2.at[1], sib)

    got(k_gsib, gx2.at[1], sib)
    for i in range(2):
        gcat[:, 2 * units * i : 2 * units * (i + 1)] = gx2[i, :, :, units:].reshape(
            slots, 2 * units
        )
        hcat[:, units * i : units * (i + 1)] = gx2[i, :, :, :units].reshape(slots, units)
    weight_grads(cpy, ct1, ct2)
    finish_cpy = write_grads(ct1, ct2, copy_gate_out, copy_up_out, copy_down_out)

    to = lax.broadcasted_iota(jnp.int32, (size, block), 0)
    fr = lax.broadcasted_iota(jnp.int32, (size, block), 1)
    match = fr == (to // 16) * 4 + ((to // 4) % 2) * per_chip + to % 4
    put_left = jnp.logical_and(match, (to // 8) % 2 == 0).astype(BF16)
    put_right = jnp.logical_and(match, (to // 8) % 2 == 1).astype(BF16)

    def pack(start, count):
        middle = start + count // 2
        both = dot(put_left, fin[:, start:middle]) + dot(put_right, fin[:, middle : start + count])
        return both.astype(BF16).reshape(experts, 16, count // 2)

    got(k_yf[1][0], rf_q.at[1, 0], xm)
    got(k_yf[1][1], rf_q.at[1, 1], xp)
    got(k_w0, rzq, zp)
    fin[:, cols_q] = (
        part[me, :, cols_q].astype(F32)
        + rf_q[1, 0].astype(F32)
        + rf_q[1, 1].astype(F32)
        + rzq[...].astype(F32)
    ).astype(BF16)
    back_send_q[...] = pack(sum_p, sum_q)
    back_q = exchange(back_send_q, back_recv_q)
    got(k_z[0], rz.at[0], zp)
    got(k_xf[0], rxf.at[0], xm)
    got(k_xf[1], rxf.at[1], xp)
    fin[:, cols_p] = (
        part[me, :, cols_p].astype(F32)
        + rz[0].astype(F32)
        + rxf[0].astype(F32)
        + rxf[1].astype(F32)
    ).astype(BF16)
    back_send_p[...] = pack(0, sum_p)
    back_p = exchange(back_send_p, back_recv_p)

    def restore(buf, start, count):
        middle = start + count // 2
        rows = buf[...].reshape(size, count // 2)
        outs[:, :, start:middle] = dot(own_left, rows).astype(BF16).reshape(2, 16, count // 2)
        outs[:, :, middle : start + count] = (
            dot(own_right, rows).astype(BF16).reshape(2, 16, count // 2)
        )

    back_q()
    restore(back_recv_q, sum_p, sum_q)
    back_p()
    restore(back_recv_p, 0, sum_p)
    k_out = fresh()
    msg(k_out, outs.at[o], o_out.at[c], sib)
    mine_out = local(outs.at[c], o_out.at[c])
    mine_out.wait()
    got(k_out, o_out.at[o], sib)
    finish_own()
    finish_cpy()
    for copy in sends:
        copy.wait_send()


def finish(o, g, u, d, cg, cu, cd, mixed, grad_in, g_out, u_out, d_out, cg_out, cu_out, cd_out, sem):
    copies = []
    pairs = ((g, g_out), (u, u_out), (d, d_out), (cg, cg_out), (cu, cu_out), (cd, cd_out))
    for i, (src, dst) in enumerate(pairs):
        copies.append(pltpu.make_async_copy(src, dst, sem.at[i]))
        copies[-1].start()
    half = o.shape[2]
    for side in range(2):
        mixed[:, half * side : half * (side + 1)] = o[side, :8, :]
        grad_in[:, half * side : half * (side + 1)] = o[side, 8:, :]
    for copy in copies:
        copy.wait()


def body(tokens, assign, copy_share, copy_plan, grad_out, w_gate, w_up, w_down):
    rows_in, width = tokens.shape
    experts = lax.axis_size("expert")
    units = w_gate.shape[2]
    half = width // 2
    full = half + LANES
    chunk = half // 7
    part_p = 3 * chunk
    per_chip = 4 * experts
    slots = 8 * per_chip
    block = 2 * per_chip
    mid = block // 2
    vmem = pltpu.VMEM
    sum_p = 5 * (chunk // 2)
    sum_q = half - sum_p
    messages = 128
    any_spec = pl.BlockSpec(memory_space=pl.ANY)
    vmem_spec = pl.BlockSpec(memory_space=pltpu.VMEM)
    o, g, u, d, cg, cu, cd = pl.pallas_call(
        functools.partial(kernel, experts, half, part_p, sum_p, chunk),
        out_shape=[
            jax.ShapeDtypeStruct((2, 16, half), BF16),
            jax.ShapeDtypeStruct(w_gate.shape, BF16),
            jax.ShapeDtypeStruct(w_up.shape, BF16),
            jax.ShapeDtypeStruct(w_down.shape, BF16),
            jax.ShapeDtypeStruct(w_gate.shape, BF16),
            jax.ShapeDtypeStruct(w_up.shape, BF16),
            jax.ShapeDtypeStruct(w_down.shape, BF16),
        ],
        in_specs=[
            any_spec,
            any_spec,
            any_spec,
            any_spec,
            any_spec,
            any_spec,
        ],
        out_specs=[any_spec] * 7,
        scratch_shapes=[
            pltpu.SMEM((2 * experts + rows_in,), jnp.int32),
            vmem((rows_in, width), BF16),
            vmem((rows_in, width), BF16),
            vmem((16, full), BF16),
            vmem((2, 16, full), BF16),
            vmem((experts, 16, part_p // 2), BF16),
            vmem((experts, 16, part_p // 2), BF16),
            vmem((experts, 16, (half - part_p) // 2 + LANES), BF16),
            vmem((experts, 16, (half - part_p) // 2 + LANES), BF16),
            vmem((experts, 16, half // 2), BF16),
            vmem((experts, 16, half // 2), BF16),
            vmem((8, block, full), BF16),
            vmem((8, block, half), BF16),
            vmem((2, half, 2 * units), BF16),
            vmem((2 * units, half), BF16),
            vmem((2, slots, 3 * units), F32),
            vmem((slots, 3 * units), F32),
            vmem((2, slots, 3 * units), BF16),
            vmem((experts, slots // experts, 3 * units), BF16),
            vmem((experts, slots // experts, 3 * units), BF16),
            vmem((2, experts, slots // experts, 3 * units), BF16),
            vmem((slots, 4 * units), BF16),
            vmem((slots, 2 * units), BF16),
            vmem((8, block, half), BF16),
            vmem((4, block, sum_p), BF16),
            vmem((2, mid, sum_p), BF16),
            vmem((2, block, sum_p), BF16),
            vmem((2, 2, mid, sum_q), BF16),
            vmem((2, 2, block, sum_q), BF16),
            vmem((block, sum_q), BF16),
            vmem((block, half), BF16),
            vmem((experts, 16, sum_p // 2), BF16),
            vmem((experts, 16, sum_p // 2), BF16),
            vmem((experts, 16, sum_q // 2), BF16),
            vmem((experts, 16, sum_q // 2), BF16),
            vmem((2, 16, half), BF16),
            vmem((2, half, 2 * units), BF16),
            vmem((2 * units, half), BF16),
            vmem((2, half, 2 * units), BF16),
            vmem((2 * units, half), BF16),
            pltpu.SemaphoreType.DMA((messages,)),
            pltpu.SemaphoreType.DMA((messages,)),
            pltpu.SemaphoreType.DMA((24,)),
        ],
        compiler_params=pltpu.CompilerParams(
            collective_id=0,
            has_side_effects=True,
            vmem_limit_bytes=42 * 1024 * 1024,
        ),
        cost_estimate=pl.CostEstimate(
            flops=6_000_000_000, bytes_accessed=30_000_000, transcendentals=32768
        ),
    )(
        jnp.concatenate([copy_plan, assign.reshape(rows_in), copy_share.reshape(experts)]),
        tokens,
        grad_out,
        w_gate,
        w_up,
        w_down,
    )
    return pl.pallas_call(
        finish,
        out_shape=[
            jax.ShapeDtypeStruct(tokens.shape, BF16),
            jax.ShapeDtypeStruct(tokens.shape, BF16),
            jax.ShapeDtypeStruct(w_gate.shape, BF16),
            jax.ShapeDtypeStruct(w_up.shape, BF16),
            jax.ShapeDtypeStruct(w_down.shape, BF16),
            jax.ShapeDtypeStruct(w_gate.shape, BF16),
            jax.ShapeDtypeStruct(w_up.shape, BF16),
            jax.ShapeDtypeStruct(w_down.shape, BF16),
        ],
        in_specs=[vmem_spec] + [any_spec] * 6,
        out_specs=[vmem_spec] * 2 + [any_spec] * 6,
        scratch_shapes=[pltpu.SemaphoreType.DMA((6,))],
        compiler_params=pltpu.CompilerParams(vmem_limit_bytes=4 * 1024 * 1024),
    )(o, g, u, d, cg, cu, cd)


def solution(mesh):
    placed = (
        P(("dp", "expert"), None),
        P(("dp", "expert"), None),
        P(("dp", "expert"), None),
        P(),
        P(("dp", "expert"), None),
        P("expert", None, "dp"),
        P("expert", None, "dp"),
        P("expert", "dp", None),
    )
    return jax.shard_map(
        body,
        mesh=mesh,
        in_specs=placed,
        out_specs=(
            P(("dp", "expert"), None),
            P(("dp", "expert"), None),
            P("expert", None, "dp"),
            P("expert", None, "dp"),
            P("expert", "dp", None),
            P("expert", None, "dp"),
            P("expert", None, "dp"),
            P("expert", "dp", None),
        ),
        check_vma=False,
    )
```

```python
import functools

import jax
import jax.numpy as jnp
from jax import lax
from jax.experimental import pallas as pl
from jax.experimental.pallas import tpu as pltpu
from jax.sharding import PartitionSpec as P

MESH = pl.DeviceIdType.MESH
BF16 = jnp.bfloat16
F32 = jnp.float32
LANES = 128


def dot(a, b):
    return jnp.dot(a, b, preferred_element_type=F32)


def dot_nt(a, b):
    return lax.dot_general(a, b, (((1,), (1,)), ((), ())), preferred_element_type=F32)


def dot_tn(a, b):
    return lax.dot_general(a, b, (((0,), (0,)), ((), ())), preferred_element_type=F32)


def kernel(
    experts,
    half,
    part_p,
    sum_p,
    chunk,
    ints_in,
    rows_in,
    w_gate,
    w_up,
    w_down,
    o_out,
    gate_out,
    up_out,
    down_out,
    copy_gate_out,
    copy_up_out,
    copy_down_out,
    ints,
    rows_ref,
    lines,
    own_send_p,
    own_recv_p,
    own_send_q,
    own_recv_q,
    cpy_send,
    cpy_recv,
    own,
    cpy,
    w1,
    wd,
    pre,
    pre_recv,
    acts,
    gx1,
    gx2s,
    gx2,
    gcat,
    hcat,
    part,
    rz,
    rxo,
    rxf,
    ro_q,
    rf_q,
    rzq,
    fin,
    back_send_p,
    back_recv_p,
    back_send_q,
    back_recv_q,
    outs,
    st1,
    st2,
    ct1,
    ct2,
    ssem,
    rsem,
    lsem,
):
    units = w1.shape[2] // 2
    full = half + LANES
    per_chip = 4 * experts
    slots = 8 * per_chip
    block = 2 * per_chip
    mid = block // 2
    steps = half // chunk
    sum_q = half - sum_p

    dp = lax.axis_index("dp")
    ex = lax.axis_index("expert")
    x = dp // 4
    z = (dp // 2) % 2
    c = dp % 2
    o = 1 - c

    def chip(dx, zz):
        return lax.rem(x + dx, 4) * 2 + zz

    me = chip(0, z)
    xp = (lax.rem(dp + 4, 16), ex)
    xm = (lax.rem(dp + 12, 16), ex)
    zp = (dp + 2 - 4 * z, ex)
    sib = (dp + 1 - 2 * c, ex)

    def peer(i, other=False):
        return (sib[0] if other else dp, lax.rem(ex + i, experts))

    used = [0]
    sends = []

    def fresh():
        used[0] += 1
        return used[0] - 1

    def msg(k, src, dst, dev):
        copy = pltpu.make_async_remote_copy(
            src_ref=src,
            dst_ref=dst,
            send_sem=ssem.at[k],
            recv_sem=rsem.at[k],
            device_id=dev,
            device_id_type=MESH,
        )
        copy.start()
        sends.append(copy)

    def got(k, ref, dev):
        pltpu.make_async_remote_copy(
            src_ref=ref,
            dst_ref=ref,
            send_sem=ssem.at[k],
            recv_sem=rsem.at[k],
            device_id=dev,
            device_id_type=MESH,
        ).wait_recv()

    used_local = [0]

    def local(src, dst):
        copy = pltpu.make_async_copy(src, dst, lsem.at[used_local[0]])
        used_local[0] += 1
        copy.start()
        return copy

    my_rows = pl.ds(pl.multiple_of(c * half, half), half)
    other_rows = pl.ds(pl.multiple_of(o * half, half), half)

    first_loads = [
        local(ints_in, ints),
        local(rows_in, rows_ref),
    ]

    barrier = pltpu.get_barrier_semaphore()
    greeted = [xp, xm, zp] + [peer(i) for i in range(1, experts)]
    greeted += [peer(i, True) for i in range(experts)]
    for dev in greeted:
        pl.semaphore_signal(barrier, inc=1, device_id=dev, device_id_type=MESH)

    weight_loads = [
        local(w_gate.at[0, my_rows, :], w1.at[0, :, pl.ds(0, units)]),
        local(w_up.at[0, my_rows, :], w1.at[0, :, pl.ds(units, units)]),
        local(w_down.at[0, :, my_rows], wd.at[pl.ds(0, units), :]),
    ]

    for load in first_loads:
        load.wait()

    size = 16 * experts
    line = lax.broadcasted_iota(jnp.int32, (16, LANES), 0)
    owned = jnp.zeros((16, LANES), jnp.int32)
    copied = jnp.zeros((16, LANES), jnp.int32)
    flags = jnp.zeros((16, LANES), F32)
    named = [ints[experts + t] for t in range(8)]
    for t in range(8):
        rank = jnp.int32(0)
        for earlier in range(t):
            rank += (named[earlier] == named[t]).astype(jnp.int32)
        holder = jnp.int32(0)
        for i in range(1, experts):
            holder += i * (ints[i] == named[t]).astype(jnp.int32)
        moved = (rank < ints[experts + 8 + named[t]]).astype(jnp.int32)
        here = line % 8 == t
        owned = jnp.where(here, named[t] * 16 + rank, owned)
        copied = jnp.where(here, moved * (holder * 16 + rank) - (1 - moved) * LANES, copied)
        flags = jnp.where(here, moved.astype(F32), flags)
    lane = lax.broadcasted_iota(jnp.int32, (16, LANES), 1) - (line // 8) * 2
    own_marks = [(lane == owned + 4 * q).astype(F32).astype(BF16)[:, :size] for q in range(4)]
    cpy_marks = [(lane == copied + 4 * q).astype(F32).astype(BF16)[:, :size] for q in range(4)]
    flags = flags.astype(BF16)

    lines[...] = jnp.concatenate(
        [rows_ref[0].astype(F32), rows_ref[1].astype(F32)], axis=0
    ).astype(BF16)
    pl.semaphore_wait(barrier, len(greeted))

    def spread(marks, side, start, count):
        total = None
        for q in range(4):
            begin = side * half + start + q * (count // 4)
            term = dot_tn(marks[q], lines[:, begin : begin + count // 4])
            total = term if total is None else total + term
        return total.astype(BF16).reshape(experts, 16, count // 4)

    def exchange(source, target):
        keys = [[fresh() for _ in range(experts)] for _ in range(2)]
        for i in range(1, experts):
            dev = peer(i)
            msg(keys[0][i], source.at[c, dev[1]], target.at[c, ex], dev)
            dev = peer(i, True)
            msg(keys[1][i], source.at[o, dev[1]], target.at[c, ex], dev)
        msg(keys[1][0], source.at[o, ex], target.at[c, ex], sib)
        target[c, ex] = source[c, ex]

        def arrive():
            for i in range(experts):
                at = lax.rem(ex + experts - i, experts)
                if i > 0:
                    got(keys[0][i], target.at[c, at], peer(i))
                got(keys[1][i], target.at[o, at], peer(i, True))

        return arrive

    for side in range(2):
        own_send_p[side] = spread(own_marks, side, 0, sum_p)
    arrive_p = exchange(own_send_p, own_recv_p)
    side_q = sum_q // 4
    marked = dot_tn(own_marks[0], flags).astype(BF16).reshape(experts, 16, LANES)
    for side in range(2):
        own_send_q[side, :, :, :side_q] = spread(own_marks, side, sum_p, sum_q)
        own_send_q[side, :, :, side_q:] = marked
    arrive_q = exchange(own_send_q, own_recv_q)
    for side in range(2):
        cpy_send[side] = spread(cpy_marks, side, 0, half)
    arrive_cpy = exchange(cpy_send, cpy_recv)
    k_w = [fresh() for _ in range(3)]
    msg(k_w[0], w_gate.at[0, other_rows, :], w1.at[1, :, pl.ds(0, units)], sib)
    msg(k_w[1], w_up.at[0, other_rows, :], w1.at[1, :, pl.ds(units, units)], sib)
    msg(k_w[2], w_down.at[0, :, other_rows], wd.at[pl.ds(units, units), :], sib)

    def places(shape, out, slot):
        to = lax.broadcasted_iota(jnp.int32, shape, out)
        fr = lax.broadcasted_iota(jnp.int32, shape, slot)
        row = ((fr // 2) % 2) * per_chip + ((fr // 16) % experts) * 4 + (fr // size) * 2 + fr % 2
        same = to == row
        return [
            jnp.logical_and(same, (fr // 4) % 4 == q).astype(F32).astype(BF16) for q in range(4)
        ]

    take = places((block, 2 * size), 0, 1)

    def collect(buf, arrived, start, count):
        part = count // 4
        rows = arrived[:, :, :, :part].reshape(2 * size, part)
        for q in range(4):
            buf[me, :, start + q * part : start + (q + 1) * part] = dot(take[q], rows).astype(BF16)

    def gather(buf, width, part_p):
        keys = [fresh() for _ in range(18)]

        def cut(q, lane, row=None):
            start, count = (0, block) if row is None else (row * mid, mid)
            if lane == 0:
                return buf.at[q, pl.ds(start, count), pl.ds(0, part_p)]
            return buf.at[q, pl.ds(start, count), pl.ds(part_p, width - part_p)]

        moves = {
            0: (me, 0, None, xp),
            1: (me, 0, None, xm),
            2: (me, 0, None, zp),
            3: (chip(3, z), 0, 0, xp),
            4: (chip(1, z), 0, 1, xm),
            5: (chip(3, z), 0, None, zp),
            6: (chip(1, z), 0, None, zp),
            7: (chip(2, z), 0, 0, zp),
            8: (chip(2, z), 0, 1, zp),
            9: (me, 1, None, zp),
            10: (me, 1, None, xp),
            11: (me, 1, None, xm),
            12: (chip(0, y), 1, None, xp),
            13: (chip(0, y), 1, None, xm),
            14: (chip(3, z), 1, 0, xp),
            15: (chip(1, z), 1, 1, xm),
            16: (chip(3, y), 1, 0, xp),
            17: (chip(1, y), 1, 1, xm),
        }
        lands = {
            0: (chip(3, z), 0, None, xm),
            1: (chip(1, z), 0, None, xp),
            2: (chip(0, y), 0, None, zp),
            3: (chip(2, z), 0, 0, xm),
            4: (chip(2, z), 0, 1, xp),
            5: (chip(3, y), 0, None, zp),
            6: (chip(1, y), 0, None, zp),
            7: (chip(2, y), 0, 0, zp),
            8: (chip(2, y), 0, 1, zp),
            9: (chip(0, y), 1, None, zp),
            10: (chip(3, z), 1, None, xm),
            11: (chip(1, z), 1, None, xp),
            12: (chip(3, y), 1, None, xm),
            13: (chip(1, y), 1, None, xp),
            14: (chip(2, z), 1, 0, xm),
            15: (chip(2, z), 1, 1, xp),
            16: (chip(2, y), 1, 0, xm),
            17: (chip(2, y), 1, 1, xp),
        }
        after = {3: 0, 5: 0, 4: 1, 6: 1, 12: 9, 13: 9, 14: 10, 15: 11, 7: 3, 8: 4, 16: 12, 17: 13}
        seen = set()

        def arrive(i):
            if i not in seen:
                seen.add(i)
                q, lane, row, dev = lands[i]
                got(keys[i], cut(q, lane, row), dev)

        def go(*numbers):
            for i in numbers:
                if i in after:
                    arrive(after[i])
                q, lane, row, dev = moves[i]
                msg(keys[i], cut(q, lane, row), cut(q, lane, row), dev)

        def all_in():
            for i in sorted(lands):
                arrive(i)

        return go, all_in

    y = 1 - z
    go_own, own_in = gather(own, full, 10 * LANES)
    go_cpy, cpy_in = gather(cpy, half, 8 * LANES)
    arrive_p()
    collect(own, own_recv_p, 0, sum_p)
    go_own(0, 1)
    arrive_q()
    collect(own, own_recv_q, sum_p, sum_q)
    own[me, :, half:] = dot(
        take[0], own_recv_q[:, :, :, side_q:].reshape(2 * size, LANES)
    ).astype(BF16)

    def copy_block():
        arrive_cpy()
        collect(cpy, cpy_recv, 0, half)

    def tokens_of(buf, cols):
        return buf[:, :per_chip, cols].reshape(slots, -1)

    def backs_of(buf, cols):
        return buf[:, per_chip:, cols].reshape(slots, -1)

    k_pre = fresh()
    k_acts = fresh()
    activations = acts.at[0]
    piece_rows = slots // experts

    def gates():
        for load in weight_loads:
            load.wait()
        got(k_w[0], w1.at[1, :, pl.ds(0, units)], sib)
        got(k_w[1], w1.at[1, :, pl.ds(units, units)], sib)
        got(k_w[2], wd.at[pl.ds(units, units), :], sib)
        own_in()
        pre[1, :, : 2 * units] = dot(tokens_of(own, slice(0, half)), w1[1])
        gh = dot_nt(backs_of(own, slice(0, half)), wd[...])
        pre[1, :, 2 * units :] = gh[:, units:]
        msg(k_pre, pre.at[1], pre_recv, sib)
        pre[0, :, : 2 * units] = dot(tokens_of(own, slice(0, half)), w1[0])
        pre[0, :, 2 * units :] = gh[:, :units]

    k_gx1 = [fresh() for _ in range(experts - 1)]
    k_gx2 = [fresh() for _ in range(experts - 1)]

    def activate():
        got(k_pre, pre_recv, sib)
        total = pre[0] + pre_recv[...]
        gate = total[:, :units]
        up = total[:, units : 2 * units]
        grad_hidden = total[:, 2 * units :]
        squash = jax.nn.sigmoid(gate)
        acts[0, :, :units] = (gate * squash * up).astype(BF16)
        acts[0, :, units : 2 * units] = (
            grad_hidden * up * squash * (1.0 + gate * (1.0 - squash))
        ).astype(BF16)
        acts[0, :, 2 * units :] = (grad_hidden * gate * squash).astype(BF16)
        msg(k_acts, activations, acts.at[1], sib)
        for i in range(1, experts):
            dev = peer(i)
            piece = pl.ds(pl.multiple_of(dev[1] * piece_rows, piece_rows), piece_rows)
            msg(k_gx1[i - 1], acts.at[0, piece, :], gx1.at[ex], dev)
        piece = pl.ds(pl.multiple_of(ex * piece_rows, piece_rows), piece_rows)
        gx1[ex] = acts[0, piece, :]

    def partials():
        got(k_acts, acts.at[1], sib)
        hcat[:, :units] = acts[0, :, :units]
        hcat[:, units:] = acts[1, :, :units]

        @pl.loop(0, steps)
        def _(step):
            cols = pl.ds(pl.multiple_of(step * chunk, chunk), chunk)
            m = dot(hcat[...], wd[:, cols])
            part[:, :per_chip, cols] = m.astype(BF16).reshape(8, per_chip, chunk)
            r = dot_nt(acts[0, :, units:], w1[0, cols, :]) + dot_nt(
                acts[1, :, units:], w1[1, cols, :]
            )
            part[:, per_chip:, cols] = r.astype(BF16).reshape(8, per_chip, chunk)

    def choose():
        for i in range(1, experts):
            got(k_gx1[i - 1], gx1.at[lax.rem(ex + experts - i, experts)], peer(i))
        for i in range(experts):
            gx2s[i] = gx1[ints[i]]
        for i in range(1, experts):
            dev = peer(i)
            msg(k_gx2[i - 1], gx2s.at[dev[1]], gx2.at[0, ex], dev)
        gx2[0, ex] = gx2s[ex]

    cols_p = pl.ds(0, sum_p)
    cols_q = pl.ds(sum_p, sum_q)
    first_rows = pl.ds(0, mid)
    last_rows = pl.ds(mid, mid)
    every = pl.ds(0, block)

    k_z = [fresh() for _ in range(4)]
    k_xo = [fresh() for _ in range(2)]
    k_xf = [fresh() for _ in range(2)]
    k_yo = [[fresh() for _ in range(2)] for _ in range(2)]
    k_yf = [[fresh() for _ in range(2)] for _ in range(2)]
    k_w0 = fresh()

    def add(ref, extra):
        ref[...] = (ref[...].astype(F32) + extra[...].astype(F32)).astype(BF16)

    def send_z(*numbers):
        for j in numbers:
            msg(k_z[j], part.at[chip(j, y), every, cols_p], rz.at[j], zp)

    def send_far(i):
        zz = (y, z)[i]
        msg(k_yo[i][0], part.at[chip(2, zz), first_rows, cols_q], ro_q.at[i, 0], xp)
        msg(k_yo[i][1], part.at[chip(2, zz), last_rows, cols_q], ro_q.at[i, 1], xm)

    def keep_weights():
        copied = own[:, :per_chip, half:full].reshape(slots, LANES).astype(F32)[:, :1]
        kept = 1.0 - copied
        gcat[:, : 2 * units] = (acts[0, :, units:].astype(F32) * kept).astype(BF16)
        gcat[:, 2 * units :] = (acts[1, :, units:].astype(F32) * kept).astype(BF16)
        hcat[...] = (hcat[...].astype(F32) * kept).astype(BF16)
        weight_grads(own, st1, st2, 0, steps)

    def weight_grads(buf, one, two, begin, end):
        @pl.loop(begin, end)
        def _(step):
            cols = pl.ds(pl.multiple_of(step * chunk, chunk), chunk)
            d = dot_tn(tokens_of(buf, cols), gcat[...]).astype(BF16)
            one[0, cols, :] = d[:, : 2 * units]
            one[1, cols, :] = d[:, 2 * units :]
            two[:, cols] = dot_tn(hcat[...], backs_of(buf, cols)).astype(BF16)

    def write_grads(one, two, g_out, u_out, d_out, begin, end):
        keys = [fresh() for _ in range(3)]
        lanes_g, lanes_u = pl.ds(0, units), pl.ds(units, units)
        start, count = begin * chunk, (end - begin) * chunk
        src = pl.ds(start, count)
        to_mine = pl.ds(pl.multiple_of(c * half + start, LANES), count)
        to_other = pl.ds(pl.multiple_of(o * half + start, LANES), count)
        msg(keys[0], one.at[1, src, lanes_g], g_out.at[0, to_mine, :], sib)
        msg(keys[1], one.at[1, src, lanes_u], u_out.at[0, to_mine, :], sib)
        msg(keys[2], two.at[lanes_u, src], d_out.at[0, :, to_mine], sib)
        mine = [
            local(one.at[0, src, lanes_g], g_out.at[0, to_mine, :]),
            local(one.at[0, src, lanes_u], u_out.at[0, to_mine, :]),
            local(two.at[lanes_g, src], d_out.at[0, :, to_mine]),
        ]

        def finish():
            for copy in mine:
                copy.wait()
            got(keys[0], g_out.at[0, to_other, :], sib)
            got(keys[1], u_out.at[0, to_other, :], sib)
            got(keys[2], d_out.at[0, :, to_other], sib)

        return finish

    def pass_on(i, right):
        zz = (y, z)[i]
        if right:
            got(k_yo[i][0], ro_q.at[i, 0], xm)
            add(part.at[chip(1, zz), first_rows, cols_q], ro_q.at[i, 0])
            msg(k_yf[i][0], part.at[chip(1, zz), every, cols_q], rf_q.at[i, 0], xp)
        else:
            got(k_yo[i][1], ro_q.at[i, 1], xp)
            add(part.at[chip(3, zz), last_rows, cols_q], ro_q.at[i, 1])
            msg(k_yf[i][1], part.at[chip(3, zz), every, cols_q], rf_q.at[i, 1], xm)

    def sum_z(j):
        got(k_z[j], rz.at[j], zp)
        add(part.at[chip(j, z), every, cols_p], rz.at[j])

    def send_opposite():
        sum_z(2)
        msg(k_xo[0], part.at[chip(2, z), first_rows, cols_p], rxo.at[0], xp)
        msg(k_xo[1], part.at[chip(2, z), last_rows, cols_p], rxo.at[1], xm)

    def send_right():
        got(k_xo[0], rxo.at[0], xm)
        add(part.at[chip(1, z), first_rows, cols_p], rxo.at[0])
        msg(k_xf[0], part.at[chip(1, z), every, cols_p], rxf.at[0], xp)

    def send_left():
        got(k_xo[1], rxo.at[1], xp)
        add(part.at[chip(3, z), last_rows, cols_p], rxo.at[1])
        msg(k_xf[1], part.at[chip(3, z), every, cols_p], rxf.at[1], xm)

    def send_last():
        got(k_yf[0][0], rf_q.at[0, 0], xm)
        got(k_yf[0][1], rf_q.at[0, 1], xp)
        mine_y = part.at[chip(0, y), every, cols_q]
        mine_y[...] = (
            mine_y[...].astype(F32) + rf_q[0, 0].astype(F32) + rf_q[0, 1].astype(F32)
        ).astype(BF16)
        msg(k_w0, mine_y, rzq, zp)

    k_gsib = fresh()

    def share_choice():
        for i in range(1, experts):
            got(k_gx2[i - 1], gx2.at[0, lax.rem(ex + experts - i, experts)], peer(i))
        msg(k_gsib, gx2.at[0], gx2.at[1], sib)

    def copy_weights():
        got(k_gsib, gx2.at[1], sib)
        cpy_in()
        for i in range(2):
            gcat[:, 2 * units * i : 2 * units * (i + 1)] = gx2[i, :, :, units:].reshape(
                slots, 2 * units
            )
            hcat[:, units * i : units * (i + 1)] = gx2[i, :, :, :units].reshape(slots, units)
        weight_grads(cpy, ct1, ct2, 0, steps)

    go_own(9, 10, 11, 3, 5, 4, 6, 12, 13, 2, 14, 15, 7, 8, 16, 17)
    copy_block()
    go_cpy(0, 1, 9, 10, 11)
    gates()
    go_cpy(3, 5, 4, 6, 12, 13, 2)
    activate()
    partials()
    send_z(2, 1, 3, 0)
    send_far(0)
    send_far(1)
    go_cpy(14, 15, 7, 8, 16, 17)
    choose()
    keep_weights()
    finish_own = write_grads(st1, st2, gate_out, up_out, down_out, 0, steps)
    pass_on(0, True)
    pass_on(0, False)
    send_opposite()
    sum_z(1)
    sum_z(3)
    pass_on(1, True)
    pass_on(1, False)
    send_right()
    send_left()
    send_last()
    share_choice()
    copy_weights()
    copy_outs = (copy_gate_out, copy_up_out, copy_down_out)
    finish_cpy = write_grads(ct1, ct2, *copy_outs, 0, steps)
    put = places((2 * size, block), 1, 0)

    def pack(start, count):
        total = None
        for q in range(4):
            begin = start + q * (count // 4)
            term = dot(put[q], fin[:, begin : begin + count // 4])
            total = term if total is None else total + term
        return total.astype(BF16).reshape(2, experts, 16, count // 4)

    got(k_yf[1][0], rf_q.at[1, 0], xm)
    got(k_yf[1][1], rf_q.at[1, 1], xp)
    got(k_w0, rzq, zp)
    fin[:, cols_q] = (
        part[me, :, cols_q].astype(F32)
        + rf_q[1, 0].astype(F32)
        + rf_q[1, 1].astype(F32)
        + rzq[...].astype(F32)
    ).astype(BF16)
    back_send_q[...] = pack(sum_p, sum_q)
    back_q = exchange(back_send_q, back_recv_q)
    got(k_z[0], rz.at[0], zp)
    got(k_xf[0], rxf.at[0], xm)
    got(k_xf[1], rxf.at[1], xp)
    fin[:, cols_p] = (
        part[me, :, cols_p].astype(F32)
        + rz[0].astype(F32)
        + rxf[0].astype(F32)
        + rxf[1].astype(F32)
    ).astype(BF16)
    back_send_p[...] = pack(0, sum_p)
    back_p = exchange(back_send_p, back_recv_p)

    def restore(buf, start, count):
        part = count // 4
        for side in range(2):
            rows = buf[side].reshape(size, part)
            for q in range(4):
                begin = start + q * part
                outs[side, :, begin : begin + part] = dot(own_marks[q], rows).astype(BF16)

    back_q()
    restore(back_recv_q, sum_p, sum_q)
    back_p()
    restore(back_recv_p, 0, sum_p)
    mine_out = local(outs, o_out)
    mine_out.wait()
    finish_own()
    finish_cpy()
    for copy in sends:
        copy.wait_send()


def finish(o, g, u, d, cg, cu, cd, mixed, grad_in, g_out, u_out, d_out, cg_out, cu_out, cd_out, sem):
    copies = []
    pairs = ((g, g_out), (u, u_out), (d, d_out), (cg, cg_out), (cu, cu_out), (cd, cd_out))
    for i, (src, dst) in enumerate(pairs):
        copies.append(pltpu.make_async_copy(src, dst, sem.at[i]))
        copies[-1].start()
    half = o.shape[2]
    for side in range(2):
        mixed[:, half * side : half * (side + 1)] = o[side, :8, :]
        grad_in[:, half * side : half * (side + 1)] = o[side, 8:, :]
    for copy in copies:
        copy.wait()


def body(tokens, assign, copy_share, copy_plan, grad_out, w_gate, w_up, w_down):
    rows_in, width = tokens.shape
    experts = lax.axis_size("expert")
    units = w_gate.shape[2]
    half = width // 2
    full = half + LANES
    chunk = half // 7
    part_p = 10 * (chunk // 4)
    per_chip = 4 * experts
    slots = 8 * per_chip
    block = 2 * per_chip
    mid = block // 2
    vmem = pltpu.VMEM
    sum_p = 12 * (chunk // 4)
    sum_q = half - sum_p
    messages = 160
    any_spec = pl.BlockSpec(memory_space=pl.ANY)
    vmem_spec = pl.BlockSpec(memory_space=pltpu.VMEM)
    o, g, u, d, cg, cu, cd = pl.pallas_call(
        functools.partial(kernel, experts, half, part_p, sum_p, chunk),
        out_shape=[
            jax.ShapeDtypeStruct((2, 16, half), BF16),
            jax.ShapeDtypeStruct(w_gate.shape, BF16),
            jax.ShapeDtypeStruct(w_up.shape, BF16),
            jax.ShapeDtypeStruct(w_down.shape, BF16),
            jax.ShapeDtypeStruct(w_gate.shape, BF16),
            jax.ShapeDtypeStruct(w_up.shape, BF16),
            jax.ShapeDtypeStruct(w_down.shape, BF16),
        ],
        in_specs=[
            any_spec,
            any_spec,
            any_spec,
            any_spec,
            any_spec,
        ],
        out_specs=[any_spec] * 7,
        scratch_shapes=[
            pltpu.SMEM((2 * experts + rows_in,), jnp.int32),
            vmem((2, rows_in, width), BF16),
            vmem((16, width), BF16),
            vmem((2, experts, 16, sum_p // 4), BF16),
            vmem((2, experts, 16, sum_p // 4), BF16),
            vmem((2, experts, 16, sum_q // 4 + LANES), BF16),
            vmem((2, experts, 16, sum_q // 4 + LANES), BF16),
            vmem((2, experts, 16, half // 4), BF16),
            vmem((2, experts, 16, half // 4), BF16),
            vmem((8, block, full), BF16),
            vmem((8, block, half), BF16),
            vmem((2, half, 2 * units), BF16),
            vmem((2 * units, half), BF16),
            vmem((2, slots, 3 * units), F32),
            vmem((slots, 3 * units), F32),
            vmem((2, slots, 3 * units), BF16),
            vmem((experts, slots // experts, 3 * units), BF16),
            vmem((experts, slots // experts, 3 * units), BF16),
            vmem((2, experts, slots // experts, 3 * units), BF16),
            vmem((slots, 4 * units), BF16),
            vmem((slots, 2 * units), BF16),
            vmem((8, block, half), BF16),
            vmem((4, block, sum_p), BF16),
            vmem((2, mid, sum_p), BF16),
            vmem((2, block, sum_p), BF16),
            vmem((2, 2, mid, sum_q), BF16),
            vmem((2, 2, block, sum_q), BF16),
            vmem((block, sum_q), BF16),
            vmem((block, half), BF16),
            vmem((2, experts, 16, sum_p // 4), BF16),
            vmem((2, experts, 16, sum_p // 4), BF16),
            vmem((2, experts, 16, sum_q // 4), BF16),
            vmem((2, experts, 16, sum_q // 4), BF16),
            vmem((2, 16, half), BF16),
            vmem((2, half, 2 * units), BF16),
            vmem((2 * units, half), BF16),
            vmem((2, half, 2 * units), BF16),
            vmem((2 * units, half), BF16),
            pltpu.SemaphoreType.DMA((messages,)),
            pltpu.SemaphoreType.DMA((messages,)),
            pltpu.SemaphoreType.DMA((24,)),
        ],
        compiler_params=pltpu.CompilerParams(
            collective_id=0,
            has_side_effects=True,
            vmem_limit_bytes=42 * 1024 * 1024,
        ),
        cost_estimate=pl.CostEstimate(
            flops=6_000_000_000, bytes_accessed=30_000_000, transcendentals=32768
        ),
    )(
        jnp.concatenate([copy_plan, assign.reshape(rows_in), copy_share.reshape(experts)]),
        jnp.stack([tokens, grad_out]),
        w_gate,
        w_up,
        w_down,
    )
    return pl.pallas_call(
        finish,
        out_shape=[
            jax.ShapeDtypeStruct(tokens.shape, BF16),
            jax.ShapeDtypeStruct(tokens.shape, BF16),
            jax.ShapeDtypeStruct(w_gate.shape, BF16),
            jax.ShapeDtypeStruct(w_up.shape, BF16),
            jax.ShapeDtypeStruct(w_down.shape, BF16),
            jax.ShapeDtypeStruct(w_gate.shape, BF16),
            jax.ShapeDtypeStruct(w_up.shape, BF16),
            jax.ShapeDtypeStruct(w_down.shape, BF16),
        ],
        in_specs=[vmem_spec] + [any_spec] * 6,
        out_specs=[vmem_spec] * 2 + [any_spec] * 6,
        scratch_shapes=[pltpu.SemaphoreType.DMA((6,))],
        compiler_params=pltpu.CompilerParams(vmem_limit_bytes=4 * 1024 * 1024),
    )(o, g, u, d, cg, cu, cd)


def solution(mesh):
    placed = (
        P(("dp", "expert"), None),
        P(("dp", "expert"), None),
        P(("dp", "expert"), None),
        P(),
        P(("dp", "expert"), None),
        P("expert", None, "dp"),
        P("expert", None, "dp"),
        P("expert", "dp", None),
    )
    return jax.shard_map(
        body,
        mesh=mesh,
        in_specs=placed,
        out_specs=(
            P(("dp", "expert"), None),
            P(("dp", "expert"), None),
            P("expert", None, "dp"),
            P("expert", None, "dp"),
            P("expert", "dp", None),
            P("expert", None, "dp"),
            P("expert", None, "dp"),
            P("expert", "dp", None),
        ),
        check_vma=False,
    )
```

```python
import functools

import jax
import jax.numpy as jnp
from jax import lax
from jax.experimental import pallas as pl
from jax.experimental.pallas import tpu as pltpu
from jax.sharding import PartitionSpec as P

MESH = pl.DeviceIdType.MESH
BF16 = jnp.bfloat16
F32 = jnp.float32
LANES = 128


def dot(a, b):
    return jnp.dot(a, b, preferred_element_type=F32)


def dot_nt(a, b):
    return lax.dot_general(a, b, (((1,), (1,)), ((), ())), preferred_element_type=F32)


def dot_tn(a, b):
    return lax.dot_general(a, b, (((0,), (0,)), ((), ())), preferred_element_type=F32)


def kernel(
    experts,
    half,
    part_p,
    sum_p,
    chunk,
    ints_in,
    rows_in,
    w_gate,
    w_up,
    w_down,
    o_out,
    gate_out,
    up_out,
    down_out,
    copy_gate_out,
    copy_up_out,
    copy_down_out,
    ints,
    rows_ref,
    lines,
    own_send_p,
    own_recv_p,
    own_send_q,
    own_recv_q,
    cpy_send,
    cpy_recv,
    own,
    cpy,
    w1,
    wd,
    pre,
    pre_recv,
    acts,
    gx1,
    gx2s,
    gx2,
    gcat,
    hcat,
    part,
    rz,
    rxo,
    rxf,
    ro_q,
    rf_q,
    rzq,
    fin,
    back_send_p,
    back_recv_p,
    back_send_q,
    back_recv_q,
    outs,
    st1,
    st2,
    ct1,
    ct2,
    ssem,
    rsem,
    lsem,
):
    units = w1.shape[2] // 2
    full = half + LANES
    per_chip = 4 * experts
    slots = 8 * per_chip
    block = 2 * per_chip
    mid = block // 2
    steps = half // chunk
    sum_q = half - sum_p

    dp = lax.axis_index("dp")
    ex = lax.axis_index("expert")
    x = dp // 4
    z = (dp // 2) % 2
    c = dp % 2
    o = 1 - c

    def chip(dx, zz):
        return lax.rem(x + dx, 4) * 2 + zz

    me = chip(0, z)
    xp = (lax.rem(dp + 4, 16), ex)
    xm = (lax.rem(dp + 12, 16), ex)
    zp = (dp + 2 - 4 * z, ex)
    sib = (dp + 1 - 2 * c, ex)

    def peer(i, other=False):
        return (sib[0] if other else dp, lax.rem(ex + i, experts))

    used = [0]
    sends = []

    def fresh():
        used[0] += 1
        return used[0] - 1

    def msg(k, src, dst, dev):
        copy = pltpu.make_async_remote_copy(
            src_ref=src,
            dst_ref=dst,
            send_sem=ssem.at[k],
            recv_sem=rsem.at[k],
            device_id=dev,
            device_id_type=MESH,
        )
        copy.start()
        sends.append(copy)

    def got(k, ref, dev):
        pltpu.make_async_remote_copy(
            src_ref=ref,
            dst_ref=ref,
            send_sem=ssem.at[k],
            recv_sem=rsem.at[k],
            device_id=dev,
            device_id_type=MESH,
        ).wait_recv()

    used_local = [0]

    def local(src, dst):
        copy = pltpu.make_async_copy(src, dst, lsem.at[used_local[0]])
        used_local[0] += 1
        copy.start()
        return copy

    my_rows = pl.ds(pl.multiple_of(c * half, half), half)
    other_rows = pl.ds(pl.multiple_of(o * half, half), half)

    first_loads = [
        local(ints_in, ints),
        local(rows_in, rows_ref),
    ]

    barrier = pltpu.get_barrier_semaphore()
    greeted = [xp, xm, zp] + [peer(i) for i in range(1, experts)]
    greeted += [peer(i, True) for i in range(experts)]
    for dev in greeted:
        pl.semaphore_signal(barrier, inc=1, device_id=dev, device_id_type=MESH)

    weight_loads = [
        local(w_gate.at[0, my_rows, :], w1.at[0, :, pl.ds(0, units)]),
        local(w_up.at[0, my_rows, :], w1.at[0, :, pl.ds(units, units)]),
        local(w_down.at[0, :, my_rows], wd.at[pl.ds(0, units), :]),
    ]

    for load in first_loads:
        load.wait()

    size = 16 * experts
    line = lax.broadcasted_iota(jnp.int32, (16, LANES), 0)
    owned = jnp.zeros((16, LANES), jnp.int32)
    targets = []
    flags = jnp.zeros((16, LANES), F32)
    named = [ints[experts + t] for t in range(8)]
    for t in range(8):
        rank = jnp.int32(0)
        for earlier in range(t):
            rank += (named[earlier] == named[t]).astype(jnp.int32)
        holder = jnp.int32(0)
        for i in range(1, experts):
            holder += i * (ints[i] == named[t]).astype(jnp.int32)
        moved = (rank < ints[experts + 8 + named[t]]).astype(jnp.int32)
        here = line % 8 == t
        targets.append(
            (named[t] * 16 + rank, moved * (holder * 16 + rank) - (1 - moved) * LANES)
        )
        owned = jnp.where(here, targets[t][0], owned)
        flags = jnp.where(here, moved.astype(F32), flags)
    lane = lax.broadcasted_iota(jnp.int32, (16, LANES), 1) - (line // 8) * 2
    cast = (size, 16)
    spot = lax.broadcasted_iota(jnp.int32, cast, 0)
    row = lax.broadcasted_iota(jnp.int32, cast, 1)
    owned_t = jnp.zeros(cast, jnp.int32)
    copied_t = jnp.zeros(cast, jnp.int32)
    for t in range(8):
        here = row % 8 == t
        owned_t = jnp.where(here, targets[t][0], owned_t)
        copied_t = jnp.where(here, targets[t][1], copied_t)
    spot = spot - (row // 8) * 2
    own_places = [(spot == owned_t + 4 * q).astype(F32).astype(BF16) for q in range(4)]
    cpy_places = [(spot == copied_t + 4 * q).astype(F32).astype(BF16) for q in range(4)]
    own_marks = [(lane == owned + 4 * q).astype(F32).astype(BF16)[:, :size] for q in range(4)]
    flags = flags.astype(BF16)

    lines[...] = jnp.concatenate(
        [rows_ref[0].astype(F32), rows_ref[1].astype(F32)], axis=0
    ).astype(BF16)

    def spread(marks, side, start, count):
        total = None
        for q in range(4):
            begin = side * half + start + q * (count // 4)
            term = dot(marks[q], lines[:, begin : begin + count // 4])
            total = term if total is None else total + term
        return total.astype(BF16).reshape(experts, 16, count // 4)

    def exchange(source, target):
        keys = [[fresh() for _ in range(experts)] for _ in range(2)]
        for i in range(1, experts):
            dev = peer(i)
            msg(keys[0][i], source.at[c, dev[1]], target.at[c, ex], dev)
            dev = peer(i, True)
            msg(keys[1][i], source.at[o, dev[1]], target.at[c, ex], dev)
        msg(keys[1][0], source.at[o, ex], target.at[c, ex], sib)
        target[c, ex] = source[c, ex]

        def arrive():
            for i in range(experts):
                at = lax.rem(ex + experts - i, experts)
                if i > 0:
                    got(keys[0][i], target.at[c, at], peer(i))
                got(keys[1][i], target.at[o, at], peer(i, True))

        return arrive

    for side in range(2):
        own_send_p[side] = spread(own_places, side, 0, sum_p)
    pl.semaphore_wait(barrier, len(greeted))
    arrive_p = exchange(own_send_p, own_recv_p)
    side_q = sum_q // 4
    marked = dot(own_places[0], flags).astype(BF16).reshape(experts, 16, LANES)
    for side in range(2):
        own_send_q[side, :, :, :side_q] = spread(own_places, side, sum_p, sum_q)
        own_send_q[side, :, :, side_q:] = marked
    arrive_q = exchange(own_send_q, own_recv_q)
    for side in range(2):
        cpy_send[side] = spread(cpy_places, side, 0, half)
    arrive_cpy = exchange(cpy_send, cpy_recv)
    k_w = [fresh() for _ in range(3)]
    msg(k_w[0], w_gate.at[0, other_rows, :], w1.at[1, :, pl.ds(0, units)], sib)
    msg(k_w[1], w_up.at[0, other_rows, :], w1.at[1, :, pl.ds(units, units)], sib)
    msg(k_w[2], w_down.at[0, :, other_rows], wd.at[pl.ds(units, units), :], sib)

    def places(shape, out, slot):
        to = lax.broadcasted_iota(jnp.int32, shape, out)
        fr = lax.broadcasted_iota(jnp.int32, shape, slot)
        row = ((fr // 2) % 2) * per_chip + ((fr // 16) % experts) * 4 + (fr // size) * 2 + fr % 2
        same = to == row
        return [
            jnp.logical_and(same, (fr // 4) % 4 == q).astype(F32).astype(BF16) for q in range(4)
        ]

    take = places((block, 2 * size), 0, 1)

    def collect(buf, arrived, start, count):
        part = count // 4
        rows = arrived[:, :, :, :part].reshape(2 * size, part)
        for q in range(4):
            buf[me, :, start + q * part : start + (q + 1) * part] = dot(take[q], rows).astype(BF16)

    def gather(buf, width, part_p):
        keys = [fresh() for _ in range(18)]

        def cut(q, lane, row=None):
            start, count = (0, block) if row is None else (row * mid, mid)
            if lane == 0:
                return buf.at[q, pl.ds(start, count), pl.ds(0, part_p)]
            return buf.at[q, pl.ds(start, count), pl.ds(part_p, width - part_p)]

        moves = {
            0: (me, 0, None, xp),
            1: (me, 0, None, xm),
            2: (me, 0, None, zp),
            3: (chip(3, z), 0, 0, xp),
            4: (chip(1, z), 0, 1, xm),
            5: (chip(3, z), 0, None, zp),
            6: (chip(1, z), 0, None, zp),
            7: (chip(2, z), 0, 0, zp),
            8: (chip(2, z), 0, 1, zp),
            9: (me, 1, None, zp),
            10: (me, 1, None, xp),
            11: (me, 1, None, xm),
            12: (chip(0, y), 1, None, xp),
            13: (chip(0, y), 1, None, xm),
            14: (chip(3, z), 1, 0, xp),
            15: (chip(1, z), 1, 1, xm),
            16: (chip(3, y), 1, 0, xp),
            17: (chip(1, y), 1, 1, xm),
        }
        lands = {
            0: (chip(3, z), 0, None, xm),
            1: (chip(1, z), 0, None, xp),
            2: (chip(0, y), 0, None, zp),
            3: (chip(2, z), 0, 0, xm),
            4: (chip(2, z), 0, 1, xp),
            5: (chip(3, y), 0, None, zp),
            6: (chip(1, y), 0, None, zp),
            7: (chip(2, y), 0, 0, zp),
            8: (chip(2, y), 0, 1, zp),
            9: (chip(0, y), 1, None, zp),
            10: (chip(3, z), 1, None, xm),
            11: (chip(1, z), 1, None, xp),
            12: (chip(3, y), 1, None, xm),
            13: (chip(1, y), 1, None, xp),
            14: (chip(2, z), 1, 0, xm),
            15: (chip(2, z), 1, 1, xp),
            16: (chip(2, y), 1, 0, xm),
            17: (chip(2, y), 1, 1, xp),
        }
        after = {3: 0, 5: 0, 4: 1, 6: 1, 12: 9, 13: 9, 14: 10, 15: 11, 7: 3, 8: 4, 16: 12, 17: 13}
        seen = set()

        def arrive(i):
            if i not in seen:
                seen.add(i)
                q, lane, row, dev = lands[i]
                got(keys[i], cut(q, lane, row), dev)

        def go(*numbers):
            for i in numbers:
                if i in after:
                    arrive(after[i])
                q, lane, row, dev = moves[i]
                msg(keys[i], cut(q, lane, row), cut(q, lane, row), dev)

        def all_in():
            for i in sorted(lands):
                arrive(i)

        return go, all_in

    y = 1 - z
    go_own, own_in = gather(own, full, 10 * LANES)
    go_cpy, cpy_in = gather(cpy, half, 8 * LANES)
    arrive_p()
    collect(own, own_recv_p, 0, sum_p)
    go_own(0, 1)
    arrive_q()
    collect(own, own_recv_q, sum_p, sum_q)
    own[me, :, half:] = dot(
        take[0], own_recv_q[:, :, :, side_q:].reshape(2 * size, LANES)
    ).astype(BF16)

    def copy_block():
        arrive_cpy()
        collect(cpy, cpy_recv, 0, half)

    def tokens_of(buf, cols):
        return buf[:, :per_chip, cols].reshape(slots, -1)

    def backs_of(buf, cols):
        return buf[:, per_chip:, cols].reshape(slots, -1)

    k_pre = fresh()
    k_acts = fresh()
    activations = acts.at[0]
    piece_rows = slots // experts

    def gates():
        for load in weight_loads:
            load.wait()
        got(k_w[0], w1.at[1, :, pl.ds(0, units)], sib)
        got(k_w[1], w1.at[1, :, pl.ds(units, units)], sib)
        got(k_w[2], wd.at[pl.ds(units, units), :], sib)
        own_in()
        pre[1, :, : 2 * units] = dot(tokens_of(own, slice(0, half)), w1[1])
        gh = dot_nt(backs_of(own, slice(0, half)), wd[...])
        pre[1, :, 2 * units :] = gh[:, units:]
        msg(k_pre, pre.at[1], pre_recv, sib)
        pre[0, :, : 2 * units] = dot(tokens_of(own, slice(0, half)), w1[0])
        pre[0, :, 2 * units :] = gh[:, :units]

    k_gx1 = [fresh() for _ in range(experts - 1)]
    k_gx2 = [fresh() for _ in range(experts - 1)]

    def activate():
        got(k_pre, pre_recv, sib)
        total = pre[0] + pre_recv[...]
        gate = total[:, :units]
        up = total[:, units : 2 * units]
        grad_hidden = total[:, 2 * units :]
        squash = jax.nn.sigmoid(gate)
        acts[0, :, :units] = (gate * squash * up).astype(BF16)
        acts[0, :, units : 2 * units] = (
            grad_hidden * up * squash * (1.0 + gate * (1.0 - squash))
        ).astype(BF16)
        acts[0, :, 2 * units :] = (grad_hidden * gate * squash).astype(BF16)
        msg(k_acts, activations, acts.at[1], sib)
        for i in range(1, experts):
            dev = peer(i)
            piece = pl.ds(pl.multiple_of(dev[1] * piece_rows, piece_rows), piece_rows)
            msg(k_gx1[i - 1], acts.at[0, piece, :], gx1.at[ex], dev)
        piece = pl.ds(pl.multiple_of(ex * piece_rows, piece_rows), piece_rows)
        gx1[ex] = acts[0, piece, :]

    def partials():
        got(k_acts, acts.at[1], sib)
        hcat[:, :units] = acts[0, :, :units]
        hcat[:, units:] = acts[1, :, :units]

        @pl.loop(0, steps)
        def _(step):
            cols = pl.ds(pl.multiple_of(step * chunk, chunk), chunk)
            m = dot(hcat[...], wd[:, cols])
            part[:, :per_chip, cols] = m.astype(BF16).reshape(8, per_chip, chunk)
            r = dot_nt(acts[0, :, units:], w1[0, cols, :]) + dot_nt(
                acts[1, :, units:], w1[1, cols, :]
            )
            part[:, per_chip:, cols] = r.astype(BF16).reshape(8, per_chip, chunk)

    def choose():
        for i in range(1, experts):
            got(k_gx1[i - 1], gx1.at[lax.rem(ex + experts - i, experts)], peer(i))
        for i in range(experts):
            gx2s[i] = gx1[ints[i]]
        for i in range(1, experts):
            dev = peer(i)
            msg(k_gx2[i - 1], gx2s.at[dev[1]], gx2.at[0, ex], dev)
        gx2[0, ex] = gx2s[ex]

    cols_p = pl.ds(0, sum_p)
    cols_q = pl.ds(sum_p, sum_q)
    first_rows = pl.ds(0, mid)
    last_rows = pl.ds(mid, mid)
    every = pl.ds(0, block)

    k_z = [fresh() for _ in range(4)]
    k_xo = [fresh() for _ in range(2)]
    k_xf = [fresh() for _ in range(2)]
    k_yo = [[fresh() for _ in range(2)] for _ in range(2)]
    k_yf = [[fresh() for _ in range(2)] for _ in range(2)]
    k_w0 = fresh()

    def add(ref, extra):
        ref[...] = (ref[...].astype(F32) + extra[...].astype(F32)).astype(BF16)

    def send_z(*numbers):
        for j in numbers:
            msg(k_z[j], part.at[chip(j, y), every, cols_p], rz.at[j], zp)

    def send_far(i):
        zz = (y, z)[i]
        msg(k_yo[i][0], part.at[chip(2, zz), first_rows, cols_q], ro_q.at[i, 0], xp)
        msg(k_yo[i][1], part.at[chip(2, zz), last_rows, cols_q], ro_q.at[i, 1], xm)

    def keep_weights():
        copied = own[:, :per_chip, half:full].reshape(slots, LANES).astype(F32)[:, :1]
        kept = 1.0 - copied
        gcat[:, : 2 * units] = (acts[0, :, units:].astype(F32) * kept).astype(BF16)
        gcat[:, 2 * units :] = (acts[1, :, units:].astype(F32) * kept).astype(BF16)
        hcat[...] = (hcat[...].astype(F32) * kept).astype(BF16)
        weight_grads(own, st1, st2, 0, steps)

    def weight_grads(buf, one, two, begin, end):
        @pl.loop(begin, end)
        def _(step):
            cols = pl.ds(pl.multiple_of(step * chunk, chunk), chunk)
            d = dot_tn(tokens_of(buf, cols), gcat[...]).astype(BF16)
            one[0, cols, :] = d[:, : 2 * units]
            one[1, cols, :] = d[:, 2 * units :]
            two[:, cols] = dot_tn(hcat[...], backs_of(buf, cols)).astype(BF16)

    def write_grads(one, two, g_out, u_out, d_out, begin, end):
        keys = [fresh() for _ in range(3)]
        lanes_g, lanes_u = pl.ds(0, units), pl.ds(units, units)
        start, count = begin * chunk, (end - begin) * chunk
        src = pl.ds(start, count)
        to_mine = pl.ds(pl.multiple_of(c * half + start, LANES), count)
        to_other = pl.ds(pl.multiple_of(o * half + start, LANES), count)
        msg(keys[0], one.at[1, src, lanes_g], g_out.at[0, to_mine, :], sib)
        msg(keys[1], one.at[1, src, lanes_u], u_out.at[0, to_mine, :], sib)
        msg(keys[2], two.at[lanes_u, src], d_out.at[0, :, to_mine], sib)
        mine = [
            local(one.at[0, src, lanes_g], g_out.at[0, to_mine, :]),
            local(one.at[0, src, lanes_u], u_out.at[0, to_mine, :]),
            local(two.at[lanes_g, src], d_out.at[0, :, to_mine]),
        ]

        def finish():
            for copy in mine:
                copy.wait()
            got(keys[0], g_out.at[0, to_other, :], sib)
            got(keys[1], u_out.at[0, to_other, :], sib)
            got(keys[2], d_out.at[0, :, to_other], sib)

        return finish

    def pass_on(i, right):
        zz = (y, z)[i]
        if right:
            got(k_yo[i][0], ro_q.at[i, 0], xm)
            add(part.at[chip(1, zz), first_rows, cols_q], ro_q.at[i, 0])
            msg(k_yf[i][0], part.at[chip(1, zz), every, cols_q], rf_q.at[i, 0], xp)
        else:
            got(k_yo[i][1], ro_q.at[i, 1], xp)
            add(part.at[chip(3, zz), last_rows, cols_q], ro_q.at[i, 1])
            msg(k_yf[i][1], part.at[chip(3, zz), every, cols_q], rf_q.at[i, 1], xm)

    def sum_z(j):
        got(k_z[j], rz.at[j], zp)
        add(part.at[chip(j, z), every, cols_p], rz.at[j])

    def send_opposite():
        sum_z(2)
        msg(k_xo[0], part.at[chip(2, z), first_rows, cols_p], rxo.at[0], xp)
        msg(k_xo[1], part.at[chip(2, z), last_rows, cols_p], rxo.at[1], xm)

    def send_right():
        got(k_xo[0], rxo.at[0], xm)
        add(part.at[chip(1, z), first_rows, cols_p], rxo.at[0])
        msg(k_xf[0], part.at[chip(1, z), every, cols_p], rxf.at[0], xp)

    def send_left():
        got(k_xo[1], rxo.at[1], xp)
        add(part.at[chip(3, z), last_rows, cols_p], rxo.at[1])
        msg(k_xf[1], part.at[chip(3, z), every, cols_p], rxf.at[1], xm)

    def send_last():
        got(k_yf[0][0], rf_q.at[0, 0], xm)
        got(k_yf[0][1], rf_q.at[0, 1], xp)
        mine_y = part.at[chip(0, y), every, cols_q]
        mine_y[...] = (
            mine_y[...].astype(F32) + rf_q[0, 0].astype(F32) + rf_q[0, 1].astype(F32)
        ).astype(BF16)
        msg(k_w0, mine_y, rzq, zp)

    k_gsib = fresh()

    def share_choice():
        for i in range(1, experts):
            got(k_gx2[i - 1], gx2.at[0, lax.rem(ex + experts - i, experts)], peer(i))
        msg(k_gsib, gx2.at[0], gx2.at[1], sib)

    def copy_weights():
        got(k_gsib, gx2.at[1], sib)
        cpy_in()
        for i in range(2):
            gcat[:, 2 * units * i : 2 * units * (i + 1)] = gx2[i, :, :, units:].reshape(
                slots, 2 * units
            )
            hcat[:, units * i : units * (i + 1)] = gx2[i, :, :, :units].reshape(slots, units)
        weight_grads(cpy, ct1, ct2, 0, steps)

    go_own(9, 10, 11, 3, 5, 4, 6, 12, 13, 2, 14, 15, 7, 8, 16, 17)
    copy_block()
    go_cpy(0, 1, 9, 10, 11)
    gates()
    activate()
    go_cpy(3, 5, 4, 6, 12, 13, 2, 14, 15, 7, 8)
    partials()
    send_z(2, 1, 3, 0)
    send_far(0)
    send_far(1)
    pass_on(0, True)
    pass_on(0, False)
    go_cpy(16, 17)
    choose()
    keep_weights()
    finish_own = write_grads(st1, st2, gate_out, up_out, down_out, 0, steps)
    send_opposite()
    sum_z(1)
    sum_z(3)
    pass_on(1, True)
    pass_on(1, False)
    send_right()
    send_left()
    send_last()
    share_choice()
    copy_weights()
    copy_outs = (copy_gate_out, copy_up_out, copy_down_out)
    finish_cpy = write_grads(ct1, ct2, *copy_outs, 0, steps)

    put = places((2 * size, block), 1, 0)

    def pack(start, count):
        total = None
        for q in range(4):
            begin = start + q * (count // 4)
            term = dot(put[q], fin[:, begin : begin + count // 4])
            total = term if total is None else total + term
        return total.astype(BF16).reshape(2, experts, 16, count // 4)

    got(k_yf[1][0], rf_q.at[1, 0], xm)
    got(k_yf[1][1], rf_q.at[1, 1], xp)
    got(k_w0, rzq, zp)
    fin[:, cols_q] = (
        part[me, :, cols_q].astype(F32)
        + rf_q[1, 0].astype(F32)
        + rf_q[1, 1].astype(F32)
        + rzq[...].astype(F32)
    ).astype(BF16)
    back_send_q[...] = pack(sum_p, sum_q)
    back_q = exchange(back_send_q, back_recv_q)
    got(k_z[0], rz.at[0], zp)
    got(k_xf[0], rxf.at[0], xm)
    got(k_xf[1], rxf.at[1], xp)
    fin[:, cols_p] = (
        part[me, :, cols_p].astype(F32)
        + rz[0].astype(F32)
        + rxf[0].astype(F32)
        + rxf[1].astype(F32)
    ).astype(BF16)
    back_send_p[...] = pack(0, sum_p)
    back_p = exchange(back_send_p, back_recv_p)

    def restore(buf, start, count):
        part = count // 4
        for side in range(2):
            rows = buf[side].reshape(size, part)
            for q in range(4):
                begin = start + q * part
                outs[side, :, begin : begin + part] = dot(own_marks[q], rows).astype(BF16)

    back_q()
    restore(back_recv_q, sum_p, sum_q)
    back_p()
    restore(back_recv_p, 0, sum_p)
    mine_out = local(outs, o_out)
    mine_out.wait()
    finish_own()
    finish_cpy()
    for copy in sends:
        copy.wait_send()


def finish(o, g, u, d, cg, cu, cd, mixed, grad_in, g_out, u_out, d_out, cg_out, cu_out, cd_out, sem):
    copies = []
    pairs = ((g, g_out), (u, u_out), (d, d_out), (cg, cg_out), (cu, cu_out), (cd, cd_out))
    for i, (src, dst) in enumerate(pairs):
        copies.append(pltpu.make_async_copy(src, dst, sem.at[i]))
        copies[-1].start()
    half = o.shape[2]
    for side in range(2):
        mixed[:, half * side : half * (side + 1)] = o[side, :8, :]
        grad_in[:, half * side : half * (side + 1)] = o[side, 8:, :]
    for copy in copies:
        copy.wait()


def body(tokens, assign, copy_share, copy_plan, grad_out, w_gate, w_up, w_down):
    rows_in, width = tokens.shape
    experts = lax.axis_size("expert")
    units = w_gate.shape[2]
    half = width // 2
    full = half + LANES
    chunk = half // 7
    part_p = 10 * (chunk // 4)
    per_chip = 4 * experts
    slots = 8 * per_chip
    block = 2 * per_chip
    mid = block // 2
    vmem = pltpu.VMEM
    sum_p = 12 * (chunk // 4)
    sum_q = half - sum_p
    messages = 160
    any_spec = pl.BlockSpec(memory_space=pl.ANY)
    vmem_spec = pl.BlockSpec(memory_space=pltpu.VMEM)
    o, g, u, d, cg, cu, cd = pl.pallas_call(
        functools.partial(kernel, experts, half, part_p, sum_p, chunk),
        out_shape=[
            jax.ShapeDtypeStruct((2, 16, half), BF16),
            jax.ShapeDtypeStruct(w_gate.shape, BF16),
            jax.ShapeDtypeStruct(w_up.shape, BF16),
            jax.ShapeDtypeStruct(w_down.shape, BF16),
            jax.ShapeDtypeStruct(w_gate.shape, BF16),
            jax.ShapeDtypeStruct(w_up.shape, BF16),
            jax.ShapeDtypeStruct(w_down.shape, BF16),
        ],
        in_specs=[
            any_spec,
            any_spec,
            any_spec,
            any_spec,
            any_spec,
        ],
        out_specs=[any_spec] * 7,
        scratch_shapes=[
            pltpu.SMEM((2 * experts + rows_in,), jnp.int32),
            vmem((2, rows_in, width), BF16),
            vmem((16, width), BF16),
            vmem((2, experts, 16, sum_p // 4), BF16),
            vmem((2, experts, 16, sum_p // 4), BF16),
            vmem((2, experts, 16, sum_q // 4 + LANES), BF16),
            vmem((2, experts, 16, sum_q // 4 + LANES), BF16),
            vmem((2, experts, 16, half // 4), BF16),
            vmem((2, experts, 16, half // 4), BF16),
            vmem((8, block, full), BF16),
            vmem((8, block, half), BF16),
            vmem((2, half, 2 * units), BF16),
            vmem((2 * units, half), BF16),
            vmem((2, slots, 3 * units), F32),
            vmem((slots, 3 * units), F32),
            vmem((2, slots, 3 * units), BF16),
            vmem((experts, slots // experts, 3 * units), BF16),
            vmem((experts, slots // experts, 3 * units), BF16),
            vmem((2, experts, slots // experts, 3 * units), BF16),
            vmem((slots, 4 * units), BF16),
            vmem((slots, 2 * units), BF16),
            vmem((8, block, half), BF16),
            vmem((4, block, sum_p), BF16),
            vmem((2, mid, sum_p), BF16),
            vmem((2, block, sum_p), BF16),
            vmem((2, 2, mid, sum_q), BF16),
            vmem((2, 2, block, sum_q), BF16),
            vmem((block, sum_q), BF16),
            vmem((block, half), BF16),
            vmem((2, experts, 16, sum_p // 4), BF16),
            vmem((2, experts, 16, sum_p // 4), BF16),
            vmem((2, experts, 16, sum_q // 4), BF16),
            vmem((2, experts, 16, sum_q // 4), BF16),
            vmem((2, 16, half), BF16),
            vmem((2, half, 2 * units), BF16),
            vmem((2 * units, half), BF16),
            vmem((2, half, 2 * units), BF16),
            vmem((2 * units, half), BF16),
            pltpu.SemaphoreType.DMA((messages,)),
            pltpu.SemaphoreType.DMA((messages,)),
            pltpu.SemaphoreType.DMA((24,)),
        ],
        compiler_params=pltpu.CompilerParams(
            collective_id=0,
            has_side_effects=True,
            vmem_limit_bytes=42 * 1024 * 1024,
        ),
        cost_estimate=pl.CostEstimate(
            flops=6_000_000_000, bytes_accessed=30_000_000, transcendentals=32768
        ),
    )(
        jnp.concatenate([copy_plan, assign.reshape(rows_in), copy_share.reshape(experts)]),
        jnp.stack([tokens, grad_out]),
        w_gate,
        w_up,
        w_down,
    )
    return pl.pallas_call(
        finish,
        out_shape=[
            jax.ShapeDtypeStruct(tokens.shape, BF16),
            jax.ShapeDtypeStruct(tokens.shape, BF16),
            jax.ShapeDtypeStruct(w_gate.shape, BF16),
            jax.ShapeDtypeStruct(w_up.shape, BF16),
            jax.ShapeDtypeStruct(w_down.shape, BF16),
            jax.ShapeDtypeStruct(w_gate.shape, BF16),
            jax.ShapeDtypeStruct(w_up.shape, BF16),
            jax.ShapeDtypeStruct(w_down.shape, BF16),
        ],
        in_specs=[vmem_spec] + [any_spec] * 6,
        out_specs=[vmem_spec] * 2 + [any_spec] * 6,
        scratch_shapes=[pltpu.SemaphoreType.DMA((6,))],
        compiler_params=pltpu.CompilerParams(vmem_limit_bytes=4 * 1024 * 1024),
    )(o, g, u, d, cg, cu, cd)


def solution(mesh):
    placed = (
        P(("dp", "expert"), None),
        P(("dp", "expert"), None),
        P(("dp", "expert"), None),
        P(),
        P(("dp", "expert"), None),
        P("expert", None, "dp"),
        P("expert", None, "dp"),
        P("expert", "dp", None),
    )
    return jax.shard_map(
        body,
        mesh=mesh,
        in_specs=placed,
        out_specs=(
            P(("dp", "expert"), None),
            P(("dp", "expert"), None),
            P("expert", None, "dp"),
            P("expert", None, "dp"),
            P("expert", "dp", None),
            P("expert", None, "dp"),
            P("expert", None, "dp"),
            P("expert", "dp", None),
        ),
        check_vma=False,
    )
```
